512 devices in a mesh: replica: 32 (over z, y_lo), fsdp: 16 (over x, y_hi, core).
Axes of the slice: x: 4, y: 4 (y_hi: 2, y_lo: 2; y = y_hi * 2 + y_lo), z: 16, core: 2. Of those that a mesh axis runs over, the one named last changes fastest.
Arguments:
- residual: bfloat16 [32, 2048, 2560], P('replica', 'fsdp'), may hold values from -6 to 6
- attention: bfloat16 [32, 2048, 2560], P('replica', 'fsdp'), may hold values from -6 to 6
- out_weight: bfloat16 [32, 2560, 2560], P('replica', None, 'fsdp'), may hold values from -6 to 6
- norm_gain: bfloat16 [32, 2560], P('replica', 'fsdp'), may hold values from 0.5 to 1.5
- cotangent: bfloat16 [32, 2048, 2560], P('replica', 'fsdp'), may hold values from -6 to 6
- step_index: int32 [1], replicated, may hold values from 0 to 63
Outputs:
- normed_out: bfloat16 [32, 2048, 2560], P('replica', 'fsdp')
- grad_residual: bfloat16 [32, 2048, 2560], P('replica', 'fsdp')
- mixed_weight: bfloat16 [32, 2560, 2560], P('replica', None, 'fsdp')
- mixed_gain: bfloat16 [32, 2560], P('replica', 'fsdp')
The draws below stay inside these ranges and needn't reach their ends.
All inputs are finite; a program needn't handle non-finite values.
Results may differ from the reference program's by a relative error of at most 0.0052.
Values may be sent and summed in bfloat16 or wider, within the bound.
A program may use at most 64 MiB of HBM per device.

```python
import math
import jax
import jax.numpy as jnp
from jax import lax

D = 2560
HEADS = 20
HEAD_DIM = 128
TOKENS = 2048
REPLICAS = 32
HOPS = 5


def raised(drawn, key, source, target, blocks, factor):
    owner, partner = [(jnp.arange(drawn.shape[axis_at]) // (drawn.shape[axis_at] // blocks)).reshape([-1 if axis == axis_at else 1 for axis in range(drawn.ndim)]) for axis_at in (source, target)]
    chosen = jax.random.permutation(key, blocks)[partner]
    strong = (owner == chosen) | (owner == (partner + blocks // 2) % blocks)
    return jnp.where(strong, factor * drawn, drawn)


def shard_levels(stream_key, extent, pieces, least, top_value):
    factor_of = 1.0
    for axis_at, parts in pieces:
        steps = jax.random.uniform(jax.random.fold_in(jax.random.fold_in(stream_key, 6), axis_at), (parts,), jnp.float32, least / len(pieces), top_value / len(pieces))
        factor_of = factor_of * jnp.repeat(jnp.exp(steps), extent[axis_at] // parts).reshape((-1,) + (1,) * (len(extent) - 1 - axis_at))
    return factor_of


def gaussian(rng, shape, spread, most, split=(), kind=jnp.bfloat16):
    values = spread * jax.random.normal(rng, shape, jnp.float32)
    if split:
        values = values * shard_levels(rng, shape, split, -0.22, 0.18)
    return jnp.clip(values, -most, most).astype(kind)


def noise_with(own_key, shape, deviation, reach, cuts, heavy, kind=jnp.bfloat16):
    values = deviation * jax.random.normal(own_key, shape, jnp.float32)
    if cuts:
        values = values * shard_levels(own_key, shape, cuts, -0.22, 0.18)
    return jnp.clip(raised(values, jax.random.fold_in(own_key, 3), *heavy), -reach, reach).astype(kind)


def setup_inputs(seed: int = 0) -> dict:
    key_list = jax.random.split(jax.random.key(seed), 7)
    residual = gaussian(key_list[0], (REPLICAS, TOKENS, D), 1.0, 6.0, ((0, 32), (1, 16)))
    attention = gaussian(key_list[1], (REPLICAS, TOKENS, HEADS * HEAD_DIM), 1.0, 6.0, ((0, 32), (1, 16)))
    out_weight = gaussian(key_list[2], (REPLICAS, HEADS * HEAD_DIM, D), 1.0, 6.0, ((0, 32), (2, 16)))
    norm_gain = jnp.clip(1.0 + 0.1 * jax.random.normal(key_list[3], (REPLICAS, D), jnp.float32), 0.5, 1.5).astype(jnp.bfloat16)
    cotangent = noise_with(key_list[4], (REPLICAS, TOKENS, D), 1.0, 6.0, ((0, 32), (1, 16)), (1, 2, 16, 2.0))
    step_index = jax.random.randint(key_list[5], (1,), 0, 64).astype(jnp.int32)
    return {"residual": residual, "attention": attention, "out_weight": out_weight, "norm_gain": norm_gain, "cotangent": cotangent, "step_index": step_index}


epsilon = 1e-05
rate_weight = 0.2
rate_gain = 0.005

def replica_update(payload):
    residual, attention, out_weight, norm_gain, cotangent = payload
    factor = 1.0 / math.sqrt(HEADS * HEAD_DIM)
    projected = (jnp.dot(attention, out_weight, preferred_element_type=jnp.float32) * factor).astype(jnp.bfloat16)
    summed = residual.astype(jnp.float32) + projected.astype(jnp.float32)
    inv_rms = lax.rsqrt(lax.optimization_barrier(jnp.mean(summed * summed, axis=-1, keepdims=True)) + epsilon)
    normed = summed * inv_rms
    gain_full = norm_gain.astype(jnp.float32)
    normed_out = (normed * gain_full).astype(jnp.bfloat16)
    cot_full = cotangent.astype(jnp.float32)
    grad_normed = cot_full * gain_full
    inner_mean = lax.optimization_barrier(jnp.mean(grad_normed * normed, axis=-1, keepdims=True))
    grad_residual = ((grad_normed - normed * inner_mean) * inv_rms).astype(jnp.bfloat16)
    grad_gain = lax.optimization_barrier(jnp.sum(cot_full * normed, axis=0))
    grad_weight = lax.dot_general(attention, grad_residual, (((0,), (0,)), ((), ())), preferred_element_type=jnp.float32) * factor
    new_weight = (out_weight.astype(jnp.float32) - rate_weight * grad_weight).astype(jnp.bfloat16)
    new_gain = (gain_full - rate_gain * grad_gain).astype(jnp.bfloat16)
    return (normed_out, grad_residual, new_weight, new_gain)

def reference(residual, attention, out_weight, norm_gain, cotangent, step_index):
    normed_out, grad_residual, new_weight, new_gain = lax.map(replica_update, (residual, attention, out_weight, norm_gain, cotangent))
    distance = jnp.left_shift(jnp.int32(1), (step_index[0] % HOPS).astype(jnp.int32))
    source = ((jnp.arange(REPLICAS, dtype=jnp.int32) - distance) % REPLICAS).astype(jnp.int32)
    partner_weight = jnp.take(new_weight, source, axis=0)
    partner_gain = jnp.take(new_gain, source, axis=0)
    mixed_weight = (0.5 * (new_weight.astype(jnp.float32) + partner_weight.astype(jnp.float32))).astype(jnp.bfloat16)
    mixed_gain = (0.5 * (new_gain.astype(jnp.float32) + partner_gain.astype(jnp.float32))).astype(jnp.bfloat16)
    return (normed_out, grad_residual, mixed_weight, mixed_gain)
```

```python
from functools import partial
import math

import jax
import jax.numpy as jnp
from jax import lax
from jax.experimental import pallas as pl
from jax.experimental.pallas import tpu as pltpu
from jax.sharding import PartitionSpec as P

EPSILON = 1e-05
RATE_WEIGHT = 0.2
RATE_GAIN = 0.005
MESH = pl.DeviceIdType.MESH
F32 = jnp.float32
BF16 = jnp.bfloat16

D = 2560
T = 128
C = 160
Q = 640
LANES = 128
CHUNK = 512
NCH = D // CHUNK


def kernel(
    distance,
    att, res, cot, weight, gain,
    normed_out, grad_out, mixed_out, mixed_gain_out,
    a, wbuf, wt, rbuf, cbuf, res_t, gn_t, pts, ptr, gts, gt, nbuf, gbuf,
    ysend, yrecv, own, new, other, mixed,
    gplace, gquad, gall, pg, pgx, pgs, pgq, ngain, ogain, mgain,
    load_sem, out_sem,
    a_send, a_recv, sib_send, sib_recv, w_send, w_recv,
    g1_send, g1_recv, g2_send, g2_recv,
    p_send, p_recv, t_send, t_recv, s1_send, s1_recv, s2_send, s2_recv,
    y_send, y_recv, z_send, z_recv, zg_send, zg_recv,
):
    r = lax.axis_index("replica")
    f = lax.axis_index("fsdp")
    replicas = lax.axis_size("replica")
    x, y, c = f // 4, (f // 2) % 2, f % 2
    s = x * 2 + c
    factor = 1.0 / math.sqrt(D)

    def at(px, py, pc, pr=r):
        return (pr, px * 4 + py * 2 + pc)

    def rx(step):
        return (x + step) % 4

    def send(src, dst, ss, rs, target):
        cp = pltpu.make_async_remote_copy(
            src_ref=src, dst_ref=dst, send_sem=ss, recv_sem=rs, device_id=target, device_id_type=MESH
        )
        cp.start()
        return cp

    def got(ref, ss, rs):
        pltpu.make_async_remote_copy(
            src_ref=ref, dst_ref=ref, send_sem=ss, recv_sem=rs, device_id=at(rx(1), y, c), device_id_type=MESH
        ).wait_recv()

    sends = []

    def rows(slot, start=0, size=T):
        return pl.ds(pl.multiple_of(slot * T + start, 64), size)

    load_a = pltpu.make_async_copy(att, a.at[rows(s)], load_sem.at[0])
    load_w = pltpu.make_async_copy(weight, wbuf, load_sem.at[1])
    load_r = pltpu.make_async_copy(res, rbuf, load_sem.at[2])
    load_c = pltpu.make_async_copy(cot, cbuf, load_sem.at[3])
    load_g = pltpu.make_async_copy(gain, gplace, load_sem.at[4])
    for cp in (load_a, load_w, load_g, load_r, load_c):
        cp.start()

    dst_r = (r + distance) % replicas
    src_r = (r + replicas - distance) % replicas
    peers = [at(rx(k), y, c) for k in (1, 2, 3)] + [at(rx(k), y, 1 - c) for k in range(4)]
    peers += [at(x, 1 - y, c), at(x, 1 - y, 1 - c), at(x, y, c, dst_r)]
    if 2 * distance != replicas:
        peers.append(at(x, y, c, src_r))
    barrier = pltpu.get_barrier_semaphore()
    for peer in peers:
        pl.semaphore_signal(barrier, inc=1, device_id=peer, device_id_type=MESH)
    load_a.wait()
    pl.semaphore_wait(barrier, len(peers))

    left, right, far = rx(3), rx(1), rx(2)
    for h in (0, 1):
        span = rows(s, 64 * h, 64)
        sends.append(send(a.at[span], a.at[span], a_send.at[0, h], a_recv.at[0, h], at(right, y, c)))
        h2 = 1 - h
        span = rows(s, 64 * h2, 64)
        sends.append(send(a.at[span], a.at[span], a_send.at[1, h2], a_recv.at[1, h2], at(left, y, c)))
    sends.append(send(a.at[rows(s)], a.at[rows(s)], sib_send.at[0], sib_recv.at[0], at(x, y, 1 - c)))

    load_w.wait()
    my_rows = pl.multiple_of(y * C, 32)
    peer_rows = pl.multiple_of((1 - y) * C, 32)

    def turn(k, _):
        k0 = pl.multiple_of(k * LANES, LANES)
        wt[pl.ds(my_rows, C), pl.ds(k0, LANES)] = wbuf[pl.ds(k0, LANES), :].T
        return 0

    lax.fori_loop(0, D // LANES, turn, 0)
    for h in (0, 1):
        span = pl.ds(pl.multiple_of(y * C + 80 * h, 16), 80)
        sends.append(send(wt.at[span], wt.at[span], w_send.at[h], w_recv.at[h], at(x, 1 - y, c)))

    load_g.wait()
    gquad[0] = gplace[...]
    quad = [at(x, y, 1 - c), at(x, 1 - y, c), at(x, 1 - y, 1 - c)]
    for i, peer in enumerate(quad):
        sends.append(send(gplace, gquad.at[1 + i], g1_send.at[i], g1_recv.at[i], peer))

    load_r.wait()
    load_c.wait()

    def turn_res(k, _):
        k0 = pl.multiple_of(k * LANES, LANES)
        res_t[pl.ds(k0, LANES), :] = rbuf[:, pl.ds(k0, LANES)].T
        return 0

    lax.fori_loop(0, D // LANES, turn_res, 0)

    for i in range(3):
        got(gquad.at[1 + i], g1_send.at[i], g1_recv.at[i])
    gall[x] = gquad[0] + gquad[1] + gquad[2] + gquad[3]
    for i, k in enumerate((1, 2, 3)):
        sends.append(send(gall.at[x], gall.at[x], g2_send.at[i], g2_recv.at[i], at(rx(k), y, c)))

    def projected(px, wrow):
        tokens = a[pl.ds(pl.multiple_of(px * 256, 256), 256), :]
        out = lax.dot_general(
            wt[pl.ds(wrow, C), :], tokens, (((1,), (1,)), ((), ())), preferred_element_type=F32
        )
        out = (out * factor).astype(BF16)
        for k in (0, 1):
            pts[px, k, pl.ds(wrow, C), :] = out[:, k * T : (k + 1) * T]

    def feature_rows(px, py, pc):
        return pl.ds(pl.multiple_of(px * Q + py * 2 * C + pc * C, 32), C)

    def hand_out(step, px, wrow, wy, i):
        for k in (0, 1):
            span = feature_rows(x, wy, c)
            src = pts.at[px, k, pl.ds(wrow, C), :]
            pc = c if k == 0 else 1 - c
            src = pts.at[px, pc, pl.ds(wrow, C), :]
            if step == 0 and k == 0:
                ptr[span, :] = src[...]
            else:
                sends.append(
                    send(src, ptr.at[span], p_send.at[step, k, i], p_recv.at[s, i], at(px, y, pc))
                )

    got(a.at[rows(x * 2 + 1 - c)], sib_send.at[0], sib_recv.at[0])
    projected(x, my_rows)
    hand_out(0, x, my_rows, y, 0)

    def forward(slot, h, i):
        span = rows(slot, 64 * h, 64)
        sends.append(send(a.at[span], a.at[span], sib_send.at[i], sib_recv.at[i], at(x, y, 1 - c)))

    def pass_on(slot, h, d, target):
        span = rows(slot, 64 * h, 64)
        sends.append(send(a.at[span], a.at[span], a_send.at[2, d], a_recv.at[2, d], target))

    got(a.at[rows(left * 2 + c, 0, 64)], a_send.at[0, 0], a_recv.at[0, 0])
    pass_on(left * 2 + c, 0, 0, at(right, y, c))
    got(a.at[rows(right * 2 + c, 64, 64)], a_send.at[1, 1], a_recv.at[1, 1])
    pass_on(right * 2 + c, 1, 1, at(left, y, c))
    forward(left * 2 + c, 0, 1)
    forward(right * 2 + c, 1, 4)

    for i, k in enumerate((3, 2, 1)):
        got(gall.at[rx(k)], g2_send.at[i], g2_recv.at[i])
    for px in range(4):
        for k in range(Q // LANES):
            k0 = px * Q + k * LANES
            row = gall[px, 0:1, k * LANES : (k + 1) * LANES].astype(F32)
            gn_t[k0 : k0 + LANES, :] = (cbuf[:, k0 : k0 + LANES].astype(F32) * row).T

    got(a.at[rows(left * 2 + c, 64, 64)], a_send.at[0, 1], a_recv.at[0, 1])
    forward(left * 2 + c, 1, 2)
    got(a.at[rows(right * 2 + c, 0, 64)], a_send.at[1, 0], a_recv.at[1, 0])
    forward(right * 2 + c, 0, 3)
    sib = 1 - c
    for h in (0, 1):
        got(a.at[rows(left * 2 + sib, 64 * h, 64)], sib_send.at[1 + h], sib_recv.at[1 + h])
    projected(left, my_rows)
    hand_out(1, left, my_rows, y, 0)
    for h in (0, 1):
        got(a.at[rows(right * 2 + sib, 64 * h, 64)], sib_send.at[3 + h], sib_recv.at[3 + h])
    projected(right, my_rows)
    hand_out(2, right, my_rows, y, 0)

    for h in (0, 1):
        span = pl.ds(pl.multiple_of((1 - y) * C + 80 * h, 16), 80)
        got(wt.at[span], w_send.at[h], w_recv.at[h])
    for step, px in ((1, left), (2, right), (0, x)):
        projected(px, peer_rows)
        hand_out(step, px, peer_rows, 1 - y, 1)
    for h in (0, 1):
        got(a.at[rows(far * 2 + c, 64 * h, 64)], a_send.at[2, h], a_recv.at[2, h])
        forward(far * 2 + c, h, 5 + h)
    for h in (0, 1):
        got(a.at[rows(far * 2 + sib, 64 * h, 64)], sib_send.at[5 + h], sib_recv.at[5 + h])
    projected(far, my_rows)
    hand_out(3, far, my_rows, y, 0)
    projected(far, peer_rows)
    hand_out(3, far, peer_rows, 1 - y, 1)

    for k in (0, 1):
        for step in range(4):
            if k == 0 and step == 0:
                continue
            px, pc = rx(step), (c if k == 0 else 1 - c)
            for i in (0, 1):
                py = y if i == 0 else 1 - y
                got(ptr.at[feature_rows(px, py, pc)], p_send.at[step, k, i], p_recv.at[px * 2 + pc, i])

    def folded(v):
        return v.reshape(LANES // 8, 8, T).sum(axis=0)

    def stats(k, carry):
        ss, gs = carry
        span = pl.ds(pl.multiple_of(k * LANES, LANES), LANES)
        sm = res_t[span, :].astype(F32) + ptr[span, :].astype(F32)
        return ss + folded(sm * sm), gs + folded(sm * gn_t[span, :])

    zero = jnp.zeros((8, T), F32)
    ss, gs = lax.fori_loop(0, D // LANES, stats, (zero, zero))
    inv = lax.rsqrt(ss.sum(axis=0, keepdims=True) * (1.0 / D) + EPSILON)
    inner = gs.sum(axis=0, keepdims=True) * (1.0 / D) * inv
    pull = inner * inv * inv

    for step in (2, 1, 3, 0):
        px = rx(step)

        def grads(k, _):
            span = pl.ds(pl.multiple_of(px * Q + k * LANES, LANES), LANES)
            sm = res_t[span, :].astype(F32) + ptr[span, :].astype(F32)
            gts[span, :] = (gn_t[span, :] * inv - sm * pull).astype(BF16)
            return 0

        lax.fori_loop(0, Q // LANES, grads, 0)
        for k in (0, 1):
            pc = c if k == 0 else 1 - c
            for py in (0, 1):
                src = gts.at[feature_rows(px, py, pc)]
                lanes = pl.ds(pl.multiple_of(s * T, T), T)
                if step == 0 and k == 0:
                    gt[py * C : (py + 1) * C, lanes] = src[...]
                else:
                    sends.append(
                        send(
                            src, gt.at[py * C : (py + 1) * C, lanes],
                            t_send.at[step, k, py], t_recv.at[s, py], at(px, y, pc),
                        )
                    )

    inv_n = jnp.broadcast_to(inv, (LANES, T)).T
    pull_n = jnp.broadcast_to(pull, (LANES, T)).T
    for px in range(4):
        for k in range(Q // LANES):
            k0 = px * Q + k * LANES
            row = gall[px, 0:1, k * LANES : (k + 1) * LANES].astype(F32)
            sm = rbuf[:, k0 : k0 + LANES].astype(F32) + ptr[k0 : k0 + LANES, :].T.astype(F32)
            ct = cbuf[:, k0 : k0 + LANES].astype(F32)
            nm = sm * inv_n
            nbuf[:, k0 : k0 + LANES] = (nm * row).astype(BF16)
            gbuf[:, k0 : k0 + LANES] = (ct * row * inv_n - sm * pull_n).astype(BF16)
            pg[px, :, k * LANES : (k + 1) * LANES] = folded(ct * nm)
    store_n = pltpu.make_async_copy(nbuf, normed_out, out_sem.at[0])
    store_g = pltpu.make_async_copy(gbuf, grad_out, out_sem.at[1])
    store_n.start()
    store_g.start()
    for i, k in enumerate((1, 2, 3)):
        px = rx(k)
        sends.append(send(pg.at[px], pgx.at[i], s1_send.at[i], s1_recv.at[i], at(px, y, c)))

    for k in (0, 1):
        for step in range(4):
            if k == 0 and step == 0:
                continue
            px, pc = rx(step), (c if k == 0 else 1 - c)
            for py in (0, 1):
                lanes = pl.ds(pl.multiple_of((px * 2 + pc) * T, T), T)
                got(gt.at[py * C : (py + 1) * C, lanes], t_send.at[step, k, py], t_recv.at[px * 2 + pc, py])

    def ycopy(j):
        return pltpu.make_async_remote_copy(
            src_ref=ysend.at[j], dst_ref=yrecv.at[j], send_sem=y_send.at[j], recv_sem=y_recv.at[j],
            device_id=at(x, 1 - y, c), device_id_type=MESH,
        )

    def zcopy(j):
        return pltpu.make_async_remote_copy(
            src_ref=new.at[j], dst_ref=other.at[j], send_sem=z_send.at[j], recv_sem=z_recv.at[j],
            device_id=at(x, y, c, dst_r), device_id_type=MESH,
        )

    def products(j, _):
        lanes = pl.ds(pl.multiple_of(j * CHUNK, CHUNK), CHUNK)
        ysend[j] = (
            jnp.dot(gt[pl.ds(peer_rows, C), :], a[:, lanes], preferred_element_type=F32) * factor
        ).astype(BF16)
        ycopy(j).start()
        own[j] = jnp.dot(gt[pl.ds(my_rows, C), :], a[:, lanes], preferred_element_type=F32) * factor
        return 0

    lax.fori_loop(0, NCH, products, 0)

    def update(j, _):
        lanes = pl.ds(pl.multiple_of(j * CHUNK, CHUNK), CHUNK)
        ycopy(j).wait()
        grad = own[j] + yrecv[j].astype(F32)
        new[j] = (wt[pl.ds(my_rows, C), lanes].astype(F32) - RATE_WEIGHT * grad).astype(BF16)
        zcopy(j).start()
        return 0

    lax.fori_loop(0, NCH, update, 0)

    for i, k in enumerate((3, 2, 1)):
        got(pgx.at[i], s1_send.at[i], s1_recv.at[i])
    pgs[...] = pg[x] + pgx[0] + pgx[1] + pgx[2]
    for i, peer in enumerate(quad):
        sends.append(send(pgs, pgq.at[i], s2_send.at[i], s2_recv.at[i], peer))
    for i in range(3):
        got(pgq.at[i], s2_send.at[i], s2_recv.at[i])
    gg = (pgs[...] + pgq[0] + pgq[1] + pgq[2]).sum(axis=0, keepdims=True)
    mgain[...] = jnp.broadcast_to(gall[x, 0:1, :].astype(F32) - RATE_GAIN * gg, mgain.shape).astype(BF16)
    window = pl.ds(pl.multiple_of((y * 2 + c) * LANES, LANES), 2 * LANES)
    ngain[...] = mgain[:, window]
    sends.append(send(ngain, ogain, zg_send, zg_recv, at(x, y, c, dst_r)))

    def mix(j, _):
        zcopy(j).wait()
        mixed[j] = (0.5 * (new[j].astype(F32) + other[j].astype(F32))).astype(BF16)
        lanes = pl.ds(pl.multiple_of(j * CHUNK, CHUNK), CHUNK)
        pltpu.make_async_copy(mixed.at[j], mixed_out.at[:, lanes], out_sem.at[2 + j]).start()
        return 0

    lax.fori_loop(0, NCH, mix, 0)
    got(ogain, zg_send, zg_recv)
    mgain[:, 0 : 2 * LANES] = (0.5 * (ngain[...].astype(F32) + ogain[...].astype(F32))).astype(BF16)
    store_m = pltpu.make_async_copy(mgain.at[:, 0 : 2 * LANES], mixed_gain_out, out_sem.at[2 + NCH])
    store_m.start()

    for cp in sends:
        cp.wait_send()
    store_n.wait()
    store_g.wait()
    store_m.wait()
    for j in range(NCH):
        lanes = pl.ds(j * CHUNK, CHUNK)
        pltpu.make_async_copy(mixed.at[j], mixed_out.at[:, lanes], out_sem.at[2 + j]).wait()


def fused(residual, attention, weight, gain_placed, cotangent, level):
    dma = pltpu.SemaphoreType.DMA
    vm = pltpu.VMEM
    scratch = [
        vm((8 * T, D), BF16),
        vm((D, C), BF16),
        vm((2 * C, D), BF16),
        vm((T, D), BF16),
        vm((T, D), BF16),
        vm((D, T), BF16),
        vm((D, T), F32),
        vm((4, 2, 2 * C, T), BF16),
        vm((D, T), BF16),
        vm((D, T), BF16),
        vm((2 * C, 8 * T), BF16),
        vm((T, D), BF16),
        vm((T, D), BF16),
        vm((NCH, C, CHUNK), BF16),
        vm((NCH, C, CHUNK), BF16),
        vm((NCH, C, CHUNK), F32),
        vm((NCH, C, CHUNK), BF16),
        vm((NCH, C, CHUNK), BF16),
        vm((NCH, C, CHUNK), BF16),
        vm((16, Q), BF16),
        vm((4, 16, Q), BF16),
        vm((4, 16, Q), BF16),
        vm((4, 8, Q), F32),
        vm((3, 8, Q), F32),
        vm((8, Q), F32),
        vm((3, 8, Q), F32),
        vm((16, 2 * LANES), BF16),
        vm((16, 2 * LANES), BF16),
        vm((16, Q), BF16),
        dma((5,)), dma((3 + NCH,)),
        dma((3, 2)), dma((3, 2)), dma((7,)), dma((7,)), dma((2,)), dma((2,)),
        dma((3,)), dma((3,)), dma((3,)), dma((3,)),
        dma((4, 2, 2)), dma((8, 2)), dma((4, 2, 2)), dma((8, 2)),
        dma((3,)), dma((3,)), dma((3,)), dma((3,)),
        dma((NCH,)), dma((NCH,)), dma((NCH,)), dma((NCH,)), dma(()), dma(()),
    ]
    hbm = pl.BlockSpec(memory_space=pl.ANY)
    return pl.pallas_call(
        partial(kernel, 2**level),
        out_shape=(
            jax.ShapeDtypeStruct((T, D), BF16),
            jax.ShapeDtypeStruct((T, D), BF16),
            jax.ShapeDtypeStruct((C, D), BF16),
            jax.ShapeDtypeStruct((16, 2 * LANES), BF16),
        ),
        in_specs=[hbm] * 5,
        out_specs=(hbm,) * 4,
        scratch_shapes=scratch,
        compiler_params=pltpu.CompilerParams(
            collective_id=level, has_side_effects=True, vmem_limit_bytes=56 * 2**20
        ),
        cost_estimate=pl.CostEstimate(flops=4 * 1024 * 320 * D, bytes_accessed=8 * 2**20, transcendentals=0),
        name=f"replica_step_{level}",
    )(attention, residual, cotangent, weight, gain_placed)


def body(residual, attention, out_weight, norm_gain, cotangent, step_index):
    f = lax.axis_index("fsdp")
    q = f % 4
    placed = jnp.zeros((Q,), BF16)
    placed = lax.dynamic_update_slice_in_dim(placed, norm_gain[0], q * C, 0)
    placed = jnp.broadcast_to(placed[None], (16, Q))
    hop_count = lax.axis_size("replica").bit_length() - 1
    args = (residual[0], attention[0], out_weight[0], placed, cotangent[0])
    branches = [
        lambda ops, level=level: fused(*ops, level) for level in range(hop_count)
    ]
    normed, grad, mixed_t, gain_window = lax.switch(step_index[0] % hop_count, branches, args)
    mixed_gain = lax.dynamic_slice_in_dim(gain_window[0], q * 32, C, 0)
    return normed[None], grad[None], mixed_t.T[None], mixed_gain[None]


def solution(mesh):
    return jax.shard_map(
        body,
        mesh=mesh,
        in_specs=(
            P("replica", "fsdp", None),
            P("replica", "fsdp", None),
            P("replica", None, "fsdp"),
            P("replica", "fsdp"),
            P("replica", "fsdp", None),
            P(),
        ),
        out_specs=(
            P("replica", "fsdp", None),
            P("replica", "fsdp", None),
            P("replica", None, "fsdp"),
            P("replica", "fsdp"),
        ),
        check_vma=False,
    )
```

```python
from functools import partial
import math

import jax
import jax.numpy as jnp
from jax import lax
from jax.experimental import pallas as pl
from jax.experimental.pallas import tpu as pltpu
from jax.sharding import PartitionSpec as P

EPSILON = 1e-05
RATE_WEIGHT = 0.2
RATE_GAIN = 0.005
MESH = pl.DeviceIdType.MESH
F32 = jnp.float32
BF16 = jnp.bfloat16

D = 2560
T = 128
C = 160
Q = 640
LANES = 128
CHUNK = 256
NCH = D // CHUNK
LONGS = {8: 2}


def kernel(
    distance, longs,
    att, res, cot, weight, gain,
    normed_out, grad_out, mixed_out, mixed_gain_out,
    a, wt, rbuf, cbuf, res_t, gn_t, pts, ptr, gts, gt, nbuf, gbuf,
    ysend, yrecv, new, other, mixed,
    gplace, gquad, gall, pg, pgx, pgs, pgq, ngain, ogain,
    load_sem, out_sem,
    a_send, a_recv, sib_send, sib_recv, w_send, w_recv,
    g1_send, g1_recv, g2_send, g2_recv,
    p_send, p_recv, t_send, t_recv, s1_send, s1_recv, s2_send, s2_recv,
    y_send, y_recv, z_send, z_recv, v_send, zg_send, zg_recv,
):
    r = lax.axis_index("replica")
    f = lax.axis_index("fsdp")
    replicas = lax.axis_size("replica")
    x, y, c = f // 4, (f // 2) % 2, f % 2
    s = x * 2 + c
    sib = 1 - c
    factor = 1.0 / math.sqrt(D)

    def at(px, py, pc, pr=r):
        return (pr, px * 4 + py * 2 + pc)

    def rx(step):
        return (x + step) % 4

    def remote(src, dst, ss, rs, target):
        return pltpu.make_async_remote_copy(
            src_ref=src, dst_ref=dst, send_sem=ss, recv_sem=rs, device_id=target, device_id_type=MESH
        )

    sends = []

    def send(src, dst, ss, rs, target):
        cp = remote(src, dst, ss, rs, target)
        cp.start()
        sends.append(cp)

    def got(ref, ss, rs):
        remote(ref, ref, ss, rs, at(rx(1), y, c)).wait_recv()

    def rows(slot, start=0, size=T):
        return pl.ds(pl.multiple_of(slot * T + start, 64), size)

    my_rows = pl.multiple_of(y * C, 32)
    peer_rows = pl.multiple_of((1 - y) * C, 32)

    def columns(py, pc, start=0, size=C):
        return pl.ds(pl.multiple_of((py * 2 + pc) * C + start, 16), size)

    load_a = pltpu.make_async_copy(att, a.at[rows(s)], load_sem.at[0])
    load_w = pltpu.make_async_copy(weight, wt.at[columns(y, c)], load_sem.at[1])
    load_r = pltpu.make_async_copy(res, rbuf, load_sem.at[2])
    load_c = pltpu.make_async_copy(cot, cbuf, load_sem.at[3])
    for cp in (load_a, load_w, load_r, load_c):
        cp.start()

    leg = (replicas - distance) // 2
    dst_r = (r + distance) % replicas
    src_r = (r + replicas - distance) % replicas
    via_r = (r + replicas - leg) % replicas
    peers = [at(rx(k), y, c) for k in (1, 2, 3)] + [at(rx(k), y, sib) for k in range(4)]
    peers += [at(x, 1 - y, c), at(x, 1 - y, sib), at(x, y, c, dst_r)]
    if 2 * distance != replicas:
        peers.append(at(x, y, c, src_r))
    if longs:
        peers += [at(x, y, c, via_r), at(x, y, c, (r + leg) % replicas)]
    barrier = pltpu.get_barrier_semaphore()
    for peer in peers:
        pl.semaphore_signal(barrier, inc=1, device_id=peer, device_id_type=MESH)

    gplace[...] = jnp.zeros(gplace.shape, F32)
    gplace[:, 0:C] = jnp.broadcast_to(gain[...].astype(F32), (8, C))
    gplace[...] = pltpu.roll(gplace[...], (y * 2 + c) * C, 1)
    gquad[0] = gplace[...]
    load_a.wait()
    load_w.wait()
    pl.semaphore_wait(barrier, len(peers))

    quad = [at(x, y, sib), at(x, 1 - y, c), at(x, 1 - y, sib)]
    for i, peer in enumerate(quad):
        send(gplace, gquad.at[1 + i], g1_send.at[i], g1_recv.at[i], peer)

    left, right, far = rx(3), rx(1), rx(2)
    for h in (0, 1):
        span = rows(s, 64 * h, 64)
        send(a.at[span], a.at[span], a_send.at[0, h], a_recv.at[0, h], at(right, y, c))
        h2 = 1 - h
        span = rows(s, 64 * h2, 64)
        send(a.at[span], a.at[span], a_send.at[1, h2], a_recv.at[1, h2], at(left, y, c))
    for h in (0, 1):
        span = columns(y, c, 80 * h, 80)
        send(wt.at[span], wt.at[span], w_send.at[h], w_recv.at[h], at(x, 1 - y, c))
    send(wt.at[columns(y, c)], wt.at[columns(y, c)], w_send.at[2], w_recv.at[2], at(x, y, sib))
    send(a.at[rows(s)], a.at[rows(s)], sib_send.at[0], sib_recv.at[0], at(x, y, sib))

    load_r.wait()
    load_c.wait()

    def turn_res(k, _):
        k0 = pl.multiple_of(k * LANES, LANES)
        res_t[pl.ds(k0, LANES), :] = rbuf[:, pl.ds(k0, LANES)].T
        return 0

    lax.fori_loop(0, D // LANES, turn_res, 0)

    for i in range(3):
        got(gquad.at[1 + i], g1_send.at[i], g1_recv.at[i])
    gall[x] = gquad[0] + gquad[1] + gquad[2] + gquad[3]
    for i, k in enumerate((1, 2, 3)):
        send(gall.at[x], gall.at[x], g2_send.at[i], g2_recv.at[i], at(rx(k), y, c))

    def projected(px, py):
        start = pl.multiple_of(py * 2 * C, 64)
        width = 512

        def part(k, total):
            depth = pl.ds(pl.multiple_of(k * width, width), width)
            return total + lax.dot_general(
                wt[pl.ds(start, 2 * C), depth], a[rows(px * 2 + c), depth], (((1,), (1,)), ((), ())),
                preferred_element_type=F32,
            )

        out = lax.fori_loop(0, D // width, part, jnp.zeros((2 * C, T), F32))
        pts[px, pl.ds(start, 2 * C), :] = (out * factor).astype(BF16)

    def feature_rows(px, py, pc):
        return pl.ds(pl.multiple_of(px * Q + py * 2 * C + pc * C, 32), C)

    def half_rows(px, py):
        return pl.ds(pl.multiple_of(px * Q + py * 2 * C, 64), 2 * C)

    def hand_out(step, px, i):
        py = y if i == 0 else 1 - y
        src = pts.at[px, pl.ds(pl.multiple_of(py * 2 * C, 64), 2 * C)]
        span = half_rows(x, py)
        if step == 0:
            ptr[span, :] = src[...]
        else:
            send(src, ptr.at[span], p_send.at[step, i], p_recv.at[x, i], at(px, y, c))

    def forward(slot, h, i):
        span = rows(slot, 64 * h, 64)
        send(a.at[span], a.at[span], sib_send.at[i], sib_recv.at[i], at(x, y, sib))

    def pass_on(slot, h, target):
        span = rows(slot, 64 * h, 64)
        send(a.at[span], a.at[span], a_send.at[2, h], a_recv.at[2, h], target)

    got(wt.at[columns(y, sib)], w_send.at[2], w_recv.at[2])
    projected(x, y)
    hand_out(0, x, 0)

    left_c, right_c, far_c = left * 2 + c, right * 2 + c, far * 2 + c
    got(a.at[rows(left_c, 0, 64)], a_send.at[0, 0], a_recv.at[0, 0])
    pass_on(left_c, 0, at(right, y, c))
    got(a.at[rows(right_c, 64, 64)], a_send.at[1, 1], a_recv.at[1, 1])
    pass_on(right_c, 1, at(left, y, c))
    forward(left_c, 0, 1)
    forward(right_c, 1, 4)
    got(a.at[rows(left_c, 64, 64)], a_send.at[0, 1], a_recv.at[0, 1])
    forward(left_c, 1, 2)
    got(a.at[rows(right_c, 0, 64)], a_send.at[1, 0], a_recv.at[1, 0])
    forward(right_c, 0, 3)

    for i, k in enumerate((3, 2, 1)):
        got(gall.at[rx(k)], g2_send.at[i], g2_recv.at[i])
    def turn_cot(n, _):
        span = pl.ds(pl.multiple_of(n * LANES, LANES), LANES)
        row = gall[n // 5, 0:1, pl.ds(pl.multiple_of(n % 5 * LANES, LANES), LANES)]
        gn_t[span, :] = (cbuf[:, span].astype(F32) * row).T
        return 0

    lax.fori_loop(0, D // LANES, turn_cot, 0)

    def near(n, _):
        projected((x + 3 + 2 * n) % 4, y)
        return 0

    lax.fori_loop(0, 2, near, 0)
    hand_out(3, left, 0)
    hand_out(1, right, 0)

    for h in (0, 1):
        span = columns(1 - y, c, 80 * h, 80)
        got(wt.at[span], w_send.at[h], w_recv.at[h])
        send(wt.at[span], wt.at[span], w_send.at[3 + h], w_recv.at[3 + h], at(x, y, sib))
    for h in (0, 1):
        got(wt.at[columns(1 - y, sib, 80 * h, 80)], w_send.at[3 + h], w_recv.at[3 + h])

    def near_again(n, _):
        projected((x + 3 + n) % 4, 1 - y)
        return 0

    lax.fori_loop(0, 3, near_again, 0)
    hand_out(3, left, 1)
    hand_out(1, right, 1)
    hand_out(0, x, 1)
    for h in (0, 1):
        got(a.at[rows(far_c, 64 * h, 64)], a_send.at[2, h], a_recv.at[2, h])

    def last(n, _):
        projected(far, (y + n) % 2)
        return 0

    lax.fori_loop(0, 2, last, 0)
    hand_out(2, far, 0)
    hand_out(2, far, 1)
    for h in (0, 1):
        forward(far_c, h, 5 + h)

    for step in (3, 1, 2):
        for i in (0, 1):
            px, py = rx(step), (y if i == 0 else 1 - y)
            got(ptr.at[half_rows(px, py)], p_send.at[step, i], p_recv.at[px, i])

    def folded(v):
        return v.reshape(LANES // 8, 8, T).sum(axis=0)

    def stats(k, carry):
        ss, gs = carry
        span = pl.ds(pl.multiple_of(k * LANES, LANES), LANES)
        sm = res_t[span, :].astype(F32) + ptr[span, :].astype(F32)
        return ss + folded(sm * sm), gs + folded(sm * gn_t[span, :])

    zero = jnp.zeros((8, T), F32)
    ss, gs = lax.fori_loop(0, D // LANES, stats, (zero, zero))
    inv = lax.rsqrt(ss.sum(axis=0, keepdims=True) * (1.0 / D) + EPSILON)
    inner = gs.sum(axis=0, keepdims=True) * (1.0 / D) * inv
    pull = inner * inv * inv

    my_lanes = pl.ds(pl.multiple_of(s * T, T), T)

    def gradient_copy(n):
        m = n % 8
        px, pc = (x + 2 + m // 2) % 4, (c + m) % 2
        py = (y + 1 + n // 8) % 2
        span = feature_rows(px, py, pc)
        land = pl.ds(pl.multiple_of(py * C, 32), C)
        cp = remote(
            gts.at[span], gt.at[land, my_lanes], t_send.at[n], t_recv.at[s, n // 8], at(px, y, pc)
        )
        return cp, span, land, m == 4

    def gradients(n, _):
        cp, span, land, mine = gradient_copy(n)
        sm = res_t[span, :].astype(F32) + ptr[span, :].astype(F32)
        gts[span, :] = (gn_t[span, :] * inv - sm * pull).astype(BF16)

        @pl.when(mine)
        def _():
            gt[land, my_lanes] = gts[span, :]

        @pl.when(jnp.logical_not(mine))
        def _():
            cp.start()

        return 0

    lax.fori_loop(0, 16, gradients, 0)

    def got_gradients(i):
        land = pl.ds(my_rows if i else peer_rows, C)
        for k in (0, 1):
            for step in range(4):
                if k == 0 and step == 0:
                    continue
                slot = rx(step) * 2 + (c if k == 0 else sib)
                lanes = pl.ds(pl.multiple_of(slot * T, T), T)
                got(gt.at[land, lanes], t_send.at[0], t_recv.at[slot, i])

    def chunk(j):
        return pl.ds(pl.multiple_of(j * CHUNK, CHUNK), CHUNK)

    def ycopy(j):
        return remote(ysend.at[j], yrecv.at[j], y_send.at[j], y_recv.at[j], at(x, 1 - y, c))

    def theirs(j, _):
        part = jnp.dot(gt[pl.ds(peer_rows, C), :], a[:, chunk(j)], preferred_element_type=F32)
        ysend[j] = (part * factor).astype(BF16)
        ycopy(j).start()
        return 0

    inv_n = jnp.broadcast_to(inv, (LANES, T)).T
    pull_n = jnp.broadcast_to(pull, (LANES, T)).T

    def token_rows(px):
        def part(k, _):
            span = pl.ds(pl.multiple_of(px * Q + k * LANES, LANES), LANES)
            within = pl.ds(pl.multiple_of(k * LANES, LANES), LANES)
            row = gall[px, 0:1, within]
            sm = rbuf[:, span].astype(F32) + ptr[span, :].T.astype(F32)
            ct = cbuf[:, span].astype(F32)
            nm = sm * inv_n
            nbuf[:, span] = (nm * row).astype(BF16)
            gbuf[:, span] = (ct * row * inv_n - sm * pull_n).astype(BF16)
            pg[px, :, within] = folded(ct * nm)
            return 0

        lax.fori_loop(0, Q // LANES, part, 0)

    store_n = pltpu.make_async_copy(nbuf, normed_out, out_sem.at[0])
    store_g = pltpu.make_async_copy(gbuf, grad_out, out_sem.at[1])

    def gain_sums():
        store_n.start()
        store_g.start()
        for i, k in enumerate((1, 2, 3)):
            px = rx(k)
            send(pg.at[px], pgx.at[i], s1_send.at[i], s1_recv.at[i], at(px, y, c))

    def gain_quad():
        for i, k in enumerate((3, 2, 1)):
            got(pgx.at[i], s1_send.at[i], s1_recv.at[i])
        pgs[...] = pg[x] + pgx[0] + pgx[1] + pgx[2]
        for i, peer in enumerate(quad):
            send(pgs, pgq.at[i], s2_send.at[i], s2_recv.at[i], peer)

    def gain_new():
        for i in range(3):
            got(pgq.at[i], s2_send.at[i], s2_recv.at[i])
        gg = (pgs[...] + pgq[0] + pgq[1] + pgq[2]).sum(axis=0, keepdims=True)
        gquad[0] = jnp.broadcast_to(gall[x, 0:1, :] - RATE_GAIN * gg, gplace.shape)
        window = pl.ds(pl.multiple_of((y * 2 + c) * LANES, LANES), 2 * LANES)
        ngain[...] = gquad[0, :, window].astype(BF16).astype(F32)
        send(ngain, ogain, zg_send, zg_recv, at(x, y, c, dst_r))

    got(a.at[rows(x * 2 + sib)], sib_send.at[0], sib_recv.at[0])
    for px, base in ((left, 1), (right, 3), (far, 5)):
        for h in (0, 1):
            got(a.at[rows(px * 2 + sib, 64 * h, 64)], sib_send.at[base + h], sib_recv.at[base + h])
    got_gradients(0)
    lax.fori_loop(0, NCH, theirs, 0)
    got_gradients(1)

    def zcopy(j):
        slot, target = j, dst_r
        if longs:
            early = j % 2 * (j < 2 * longs)
            slot = j + early * (NCH + j // 2 - j)
            target = dst_r + early * (via_r - dst_r)
        return remote(new.at[j], other.at[slot], z_send.at[j], z_recv.at[slot], at(x, y, c, target))

    def update(j):
        part = jnp.dot(gt[pl.ds(my_rows, C), :], a[:, chunk(j)], preferred_element_type=F32)
        ycopy(j).wait()
        grad = part * factor + yrecv[j].astype(F32)
        new[j] = (wt[columns(y, c), chunk(j)].astype(F32) - RATE_WEIGHT * grad).astype(BF16)
        zcopy(j).start()

    def update_beside(j, _):
        update(j)
        token_rows(j)
        return 0

    def update_alone(j, _):
        update(j)
        return 0

    lax.fori_loop(0, 4, update_beside, 0)
    gain_sums()
    lax.fori_loop(4, 7, update_alone, 0)
    gain_quad()
    lax.fori_loop(7, NCH, update_alone, 0)
    gain_new()

    for i in range(longs):
        got(other.at[NCH + i], z_send.at[0], z_recv.at[NCH + i])
        j = 2 * i + 1
        send(other.at[NCH + i], other.at[j], v_send.at[i], z_recv.at[j], at(x, y, c, via_r))

    def store_mixed(j):
        return pltpu.make_async_copy(mixed.at[j], mixed_out.at[:, chunk(j)], out_sem.at[2 + j])

    def mix(n, _):
        j = (n + 4) % NCH
        got(other.at[j], z_send.at[0], z_recv.at[j])
        mixed[j] = (0.5 * (new[j].astype(F32) + other[j].astype(F32))).astype(BF16)
        store_mixed(j).start()
        return 0

    lax.fori_loop(0, NCH, mix, 0)
    got(ogain, zg_send, zg_recv)
    mean = 0.5 * (ngain[...] + ogain[...])
    turned = pltpu.roll(mean, (2 * LANES - (y * 2 + c) * 32) % (2 * LANES), 1)
    mixed_gain_out[...] = turned[0:1, 0:C].astype(BF16)

    def sent(n, _):
        cp, _, _, mine = gradient_copy(n)

        @pl.when(jnp.logical_not(mine))
        def _():
            cp.wait_send()

        return 0

    lax.fori_loop(0, 16, sent, 0)

    def finished(j, _):
        zcopy(j).wait_send()
        store_mixed(j).wait()
        return 0

    lax.fori_loop(0, NCH, finished, 0)
    store_n.wait()
    store_g.wait()
    for cp in sends:
        cp.wait_send()


def fused(residual, attention, weight, gain, cotangent, level):
    longs = LONGS.get(2**level, 0)
    dma = pltpu.SemaphoreType.DMA
    vm = pltpu.VMEM
    scratch = [
        vm((8 * T, D), BF16),
        vm((Q, D), BF16),
        vm((T, D), BF16),
        vm((T, D), BF16),
        vm((D, T), BF16),
        vm((D, T), F32),
        vm((4, Q, T), BF16),
        vm((D, T), BF16),
        vm((D, T), BF16),
        vm((2 * C, 8 * T), BF16),
        vm((T, D), BF16),
        vm((T, D), BF16),
        vm((NCH, C, CHUNK), BF16),
        vm((NCH, C, CHUNK), BF16),
        vm((NCH, C, CHUNK), BF16),
        vm((NCH + longs, C, CHUNK), BF16),
        vm((NCH, C, CHUNK), BF16),
        vm((8, Q), F32),
        vm((4, 8, Q), F32),
        vm((4, 8, Q), F32),
        vm((4, 8, Q), F32),
        vm((3, 8, Q), F32),
        vm((8, Q), F32),
        vm((3, 8, Q), F32),
        vm((8, 2 * LANES), F32),
        vm((8, 2 * LANES), F32),
        dma((4,)), dma((2 + NCH,)),
        dma((3, 2)), dma((3, 2)), dma((7,)), dma((7,)), dma((5,)), dma((5,)),
        dma((3,)), dma((3,)), dma((3,)), dma((3,)),
        dma((4, 2)), dma((4, 2)), dma((16,)), dma((8, 2)),
        dma((3,)), dma((3,)), dma((3,)), dma((3,)),
        dma((NCH,)), dma((NCH,)), dma((NCH,)), dma((NCH + longs,)),
        dma((max(longs, 1),)), dma(()), dma(()),
    ]
    hbm = pl.BlockSpec(memory_space=pl.ANY)
    vmem = pl.BlockSpec(memory_space=pltpu.VMEM)
    return pl.pallas_call(
        partial(kernel, 2**level, longs),
        out_shape=(
            jax.ShapeDtypeStruct((T, D), BF16),
            jax.ShapeDtypeStruct((T, D), BF16),
            jax.ShapeDtypeStruct((C, D), BF16),
            jax.ShapeDtypeStruct((1, C), BF16),
        ),
        in_specs=[hbm] * 4 + [vmem],
        out_specs=(hbm, hbm, hbm, vmem),
        scratch_shapes=scratch,
        compiler_params=pltpu.CompilerParams(
            collective_id=level, has_side_effects=True, vmem_limit_bytes=56 * 2**20
        ),
        cost_estimate=pl.CostEstimate(flops=4 * 1024 * 320 * D, bytes_accessed=8 * 2**20, transcendentals=0),
        name=f"replica_step_{level}",
    )(attention, residual, cotangent, weight, gain)


def body(residual, attention, out_weight, norm_gain, cotangent, step_index):
    hop_count = lax.axis_size("replica").bit_length() - 1
    args = (residual[0], attention[0], out_weight[0].T, norm_gain, cotangent[0])
    branches = [lambda ops, level=level: fused(*ops, level) for level in range(hop_count)]
    normed, grad, mixed_t, mixed_gain = lax.switch(step_index[0] % hop_count, branches, args)
    return normed[None], grad[None], mixed_t.T[None], mixed_gain


def solution(mesh):
    return jax.shard_map(
        body,
        mesh=mesh,
        in_specs=(
            P("replica", "fsdp", None),
            P("replica", "fsdp", None),
            P("replica", None, "fsdp"),
            P("replica", "fsdp"),
            P("replica", "fsdp", None),
            P(),
        ),
        out_specs=(
            P("replica", "fsdp", None),
            P("replica", "fsdp", None),
            P("replica", None, "fsdp"),
            P("replica", "fsdp"),
        ),
        check_vma=False,
    )
```

```python
from functools import partial
import math

import jax
import jax.numpy as jnp
from jax import lax
from jax.experimental import pallas as pl
from jax.experimental.pallas import tpu as pltpu
from jax.sharding import PartitionSpec as P

EPSILON = 1e-05
RATE_WEIGHT = 0.2
RATE_GAIN = 0.005
MESH = pl.DeviceIdType.MESH
F32 = jnp.float32
BF16 = jnp.bfloat16

D = 2560
T = 128
C = 160
Q = 640
LANES = 128
CHUNK = 256
NCH = D // CHUNK
LONGS = {8: 2}


def kernel(
    distance, longs,
    att, res, cot, weight, gain,
    normed_out, grad_out, mixed_out, mixed_gain_out,
    gain_in, a, wt, rbuf, cbuf, res_t, gn_t, pts, ptr, gts, gt, nbuf, gbuf,
    ysend, yrecv, new, other, mixed,
    gplace, gquad, gall, pg, pgx, pgs, pgq, ngain, ogain,
    load_sem, out_sem,
    a_send, a_recv, sib_send, sib_recv, w_send, w_recv,
    g1_send, g1_recv, g2_send, g2_recv,
    p_send, p_recv, t_send, t_recv, s1_send, s1_recv, s2_send, s2_recv,
    y_send, y_recv, z_send, z_recv, v_send, zg_send, zg_recv,
):
    r = lax.axis_index("replica")
    f = lax.axis_index("fsdp")
    replicas = lax.axis_size("replica")
    x, y, c = f // 4, (f // 2) % 2, f % 2
    s = x * 2 + c
    sib = 1 - c
    factor = 1.0 / math.sqrt(D)

    def at(px, py, pc, pr=r):
        return (pr, px * 4 + py * 2 + pc)

    def rx(step):
        return (x + step) % 4

    def remote(src, dst, ss, rs, target):
        return pltpu.make_async_remote_copy(
            src_ref=src, dst_ref=dst, send_sem=ss, recv_sem=rs, device_id=target, device_id_type=MESH
        )

    sends = []

    def send(src, dst, ss, rs, target):
        cp = remote(src, dst, ss, rs, target)
        cp.start()
        sends.append(cp)

    def got(ref, ss, rs):
        remote(ref, ref, ss, rs, at(rx(1), y, c)).wait_recv()

    def rows(slot, start=0, size=T):
        return pl.ds(pl.multiple_of(slot * T + start, 64), size)

    my_rows = pl.multiple_of(y * C, 32)
    peer_rows = pl.multiple_of((1 - y) * C, 32)

    def columns(py, pc, start=0, size=C):
        return pl.ds(pl.multiple_of((py * 2 + pc) * C + start, 16), size)

    load_a = pltpu.make_async_copy(att, a.at[rows(s)], load_sem.at[0])
    load_w = pltpu.make_async_copy(weight, wt.at[columns(y, c)], load_sem.at[1])
    load_r = pltpu.make_async_copy(res, rbuf, load_sem.at[2])
    load_c = pltpu.make_async_copy(cot, cbuf, load_sem.at[3])
    load_g = pltpu.make_async_copy(gain, gain_in, load_sem.at[4])
    for cp in (load_g, load_a, load_w, load_r, load_c):
        cp.start()

    leg = (replicas - distance) // 2
    dst_r = (r + distance) % replicas
    src_r = (r + replicas - distance) % replicas
    via_r = (r + replicas - leg) % replicas
    peers = [at(rx(k), y, c) for k in (1, 2, 3)] + [at(rx(k), y, sib) for k in range(4)]
    peers += [at(x, 1 - y, c), at(x, 1 - y, sib), at(x, y, c, dst_r)]
    if 2 * distance != replicas:
        peers.append(at(x, y, c, src_r))
    if longs:
        peers += [at(x, y, c, via_r), at(x, y, c, (r + leg) % replicas)]
    barrier = pltpu.get_barrier_semaphore()
    for peer in peers:
        pl.semaphore_signal(barrier, inc=1, device_id=peer, device_id_type=MESH)

    gplace[...] = jnp.zeros(gplace.shape, F32)
    load_g.wait()
    gplace[:, 0:C] = jnp.broadcast_to(gain_in[...].astype(F32), (8, C))
    gplace[...] = pltpu.roll(gplace[...], (y * 2 + c) * C, 1)
    gquad[0] = gplace[...]
    load_a.wait()
    load_w.wait()
    pl.semaphore_wait(barrier, len(peers))

    quad = [at(x, y, sib), at(x, 1 - y, c), at(x, 1 - y, sib)]
    for i, peer in enumerate(quad):
        send(gplace, gquad.at[1 + i], g1_send.at[i], g1_recv.at[i], peer)

    left, right, far = rx(3), rx(1), rx(2)
    for h in (0, 1):
        span = rows(s, 64 * h, 64)
        send(a.at[span], a.at[span], a_send.at[0, h], a_recv.at[0, h], at(right, y, c))
        h2 = 1 - h
        span = rows(s, 64 * h2, 64)
        send(a.at[span], a.at[span], a_send.at[1, h2], a_recv.at[1, h2], at(left, y, c))
    for h in (0, 1):
        span = columns(y, c, 80 * h, 80)
        send(wt.at[span], wt.at[span], w_send.at[h], w_recv.at[h], at(x, 1 - y, c))
    send(wt.at[columns(y, c)], wt.at[columns(y, c)], w_send.at[2], w_recv.at[2], at(x, y, sib))
    send(a.at[rows(s)], a.at[rows(s)], sib_send.at[0], sib_recv.at[0], at(x, y, sib))

    load_r.wait()
    load_c.wait()

    def turn_res(k, _):
        k0 = pl.multiple_of(k * LANES, LANES)
        res_t[pl.ds(k0, LANES), :] = rbuf[:, pl.ds(k0, LANES)].T
        return 0

    lax.fori_loop(0, D // LANES, turn_res, 0)

    for i in range(3):
        got(gquad.at[1 + i], g1_send.at[i], g1_recv.at[i])
    gall[x] = gquad[0] + gquad[1] + gquad[2] + gquad[3]
    for i, k in enumerate((1, 2, 3)):
        send(gall.at[x], gall.at[x], g2_send.at[i], g2_recv.at[i], at(rx(k), y, c))

    def projected(px, py):
        start = pl.multiple_of(py * 2 * C, 64)
        out = lax.dot_general(
            wt[pl.ds(start, 2 * C), :], a[rows(px * 2 + c), :], (((1,), (1,)), ((), ())),
            preferred_element_type=F32,
        )
        pts[px, pl.ds(start, 2 * C), :] = (out * factor).astype(BF16)

    def feature_rows(px, py, pc):
        return pl.ds(pl.multiple_of(px * Q + py * 2 * C + pc * C, 32), C)

    def half_rows(px, py):
        return pl.ds(pl.multiple_of(px * Q + py * 2 * C, 64), 2 * C)

    def hand_out(step, px, i):
        py = y if i == 0 else 1 - y
        src = pts.at[px, pl.ds(pl.multiple_of(py * 2 * C, 64), 2 * C)]
        span = half_rows(x, py)
        if step == 0:
            ptr[span, :] = src[...]
        else:
            send(src, ptr.at[span], p_send.at[step, i], p_recv.at[x, i], at(px, y, c))

    def forward(slot, h, i):
        span = rows(slot, 64 * h, 64)
        send(a.at[span], a.at[span], sib_send.at[i], sib_recv.at[i], at(x, y, sib))

    def pass_on(slot, h, target):
        span = rows(slot, 64 * h, 64)
        send(a.at[span], a.at[span], a_send.at[2, h], a_recv.at[2, h], target)

    got(wt.at[columns(y, sib)], w_send.at[2], w_recv.at[2])
    projected(x, y)
    hand_out(0, x, 0)

    left_c, right_c, far_c = left * 2 + c, right * 2 + c, far * 2 + c
    got(a.at[rows(left_c, 0, 64)], a_send.at[0, 0], a_recv.at[0, 0])
    pass_on(left_c, 0, at(right, y, c))
    got(a.at[rows(right_c, 64, 64)], a_send.at[1, 1], a_recv.at[1, 1])
    pass_on(right_c, 1, at(left, y, c))
    forward(left_c, 0, 1)
    forward(right_c, 1, 4)
    got(a.at[rows(left_c, 64, 64)], a_send.at[0, 1], a_recv.at[0, 1])
    forward(left_c, 1, 2)
    got(a.at[rows(right_c, 0, 64)], a_send.at[1, 0], a_recv.at[1, 0])
    forward(right_c, 0, 3)

    for i, k in enumerate((3, 2, 1)):
        got(gall.at[rx(k)], g2_send.at[i], g2_recv.at[i])
    def turn_cot(n, _):
        span = pl.ds(pl.multiple_of(n * LANES, LANES), LANES)
        row = gall[n // 5, 0:1, pl.ds(pl.multiple_of(n % 5 * LANES, LANES), LANES)]
        gn_t[span, :] = (cbuf[:, span].astype(F32) * row).T
        return 0

    lax.fori_loop(0, D // LANES, turn_cot, 0)

    def near(n, _):
        projected((x + 3 + 2 * n) % 4, y)
        return 0

    lax.fori_loop(0, 2, near, 0)
    hand_out(3, left, 0)
    hand_out(1, right, 0)

    for h in (0, 1):
        span = columns(1 - y, c, 80 * h, 80)
        got(wt.at[span], w_send.at[h], w_recv.at[h])
        send(wt.at[span], wt.at[span], w_send.at[3 + h], w_recv.at[3 + h], at(x, y, sib))
    for h in (0, 1):
        got(wt.at[columns(1 - y, sib, 80 * h, 80)], w_send.at[3 + h], w_recv.at[3 + h])

    def near_again(n, _):
        projected((x + 3 + n) % 4, 1 - y)
        return 0

    lax.fori_loop(0, 3, near_again, 0)
    hand_out(3, left, 1)
    hand_out(1, right, 1)
    hand_out(0, x, 1)
    for h in (0, 1):
        got(a.at[rows(far_c, 64 * h, 64)], a_send.at[2, h], a_recv.at[2, h])

    projected(far, y)
    hand_out(2, far, 0)
    projected(far, 1 - y)
    hand_out(2, far, 1)
    for h in (0, 1):
        forward(far_c, h, 5 + h)

    def folded(v):
        return v.reshape(LANES // 8, 8, T).sum(axis=0)

    def stats(n, carry):
        ss, gs = carry
        span = pl.ds(pl.multiple_of((x + 3 + n // 5) % 4 * Q + n % 5 * LANES, LANES), LANES)
        sm = res_t[span, :].astype(F32) + ptr[span, :].astype(F32)
        return ss + folded(sm * sm), gs + folded(sm * gn_t[span, :])

    def got_features(step):
        for i in (0, 1):
            px, py = rx(step), (y if i == 0 else 1 - y)
            got(ptr.at[half_rows(px, py)], p_send.at[step, i], p_recv.at[px, i])

    zero = jnp.zeros((8, T), F32)
    got_features(3)
    got_features(1)
    sums = lax.fori_loop(0, 15, stats, (zero, zero))
    got_features(2)
    ss, gs = lax.fori_loop(15, 20, stats, sums)
    inv = lax.rsqrt(ss.sum(axis=0, keepdims=True) * (1.0 / D) + EPSILON)
    inner = gs.sum(axis=0, keepdims=True) * (1.0 / D) * inv
    pull = inner * inv * inv

    my_lanes = pl.ds(pl.multiple_of(s * T, T), T)

    def gradient_copy(n):
        m = n % 8
        px, pc = (x + 2 + m // 2) % 4, (c + m) % 2
        py = (y + 1 + n // 8) % 2
        span = feature_rows(px, py, pc)
        land = pl.ds(pl.multiple_of(py * C, 32), C)
        cp = remote(
            gts.at[span], gt.at[land, my_lanes], t_send.at[n], t_recv.at[s, n // 8], at(px, y, pc)
        )
        return cp, span, land, m == 4

    def gradients(n, _):
        cp, span, land, mine = gradient_copy(n)
        sm = res_t[span, :].astype(F32) + ptr[span, :].astype(F32)
        gts[span, :] = (gn_t[span, :] * inv - sm * pull).astype(BF16)

        @pl.when(mine)
        def _():
            gt[land, my_lanes] = gts[span, :]

        @pl.when(jnp.logical_not(mine))
        def _():
            cp.start()

        return 0

    lax.fori_loop(0, 16, gradients, 0)

    def got_gradients(i):
        land = pl.ds(my_rows if i else peer_rows, C)
        for k in (0, 1):
            for step in range(4):
                if k == 0 and step == 0:
                    continue
                slot = rx(step) * 2 + (c if k == 0 else sib)
                lanes = pl.ds(pl.multiple_of(slot * T, T), T)
                got(gt.at[land, lanes], t_send.at[0], t_recv.at[slot, i])

    def chunk(j):
        return pl.ds(pl.multiple_of(j * CHUNK, CHUNK), CHUNK)

    def ycopy(j):
        return remote(ysend.at[j], yrecv.at[j], y_send.at[j], y_recv.at[j], at(x, 1 - y, c))

    def theirs(j, _):
        part = jnp.dot(gt[pl.ds(peer_rows, C), :], a[:, chunk(j)], preferred_element_type=F32)
        ysend[j] = (part * factor).astype(BF16)
        ycopy(j).start()
        return 0

    inv_n = jnp.broadcast_to(inv, (LANES, T)).T
    pull_n = jnp.broadcast_to(pull, (LANES, T)).T

    def token_rows(px):
        def part(k, _):
            span = pl.ds(pl.multiple_of(px * Q + k * LANES, LANES), LANES)
            within = pl.ds(pl.multiple_of(k * LANES, LANES), LANES)
            row = gall[px, 0:1, within]
            sm = rbuf[:, span].astype(F32) + ptr[span, :].T.astype(F32)
            ct = cbuf[:, span].astype(F32)
            nm = sm * inv_n
            nbuf[:, span] = (nm * row).astype(BF16)
            gbuf[:, span] = (ct * row * inv_n - sm * pull_n).astype(BF16)
            pg[px, :, within] = folded(ct * nm)
            return 0

        lax.fori_loop(0, Q // LANES, part, 0)

    store_n = pltpu.make_async_copy(nbuf, normed_out, out_sem.at[0])
    store_g = pltpu.make_async_copy(gbuf, grad_out, out_sem.at[1])

    def gain_sums():
        store_n.start()
        store_g.start()
        for i, k in enumerate((1, 2, 3)):
            px = rx(k)
            send(pg.at[px], pgx.at[i], s1_send.at[i], s1_recv.at[i], at(px, y, c))

    def gain_quad():
        for i, k in enumerate((3, 2, 1)):
            got(pgx.at[i], s1_send.at[i], s1_recv.at[i])
        pgs[...] = pg[x] + pgx[0] + pgx[1] + pgx[2]
        for i, peer in enumerate(quad):
            send(pgs, pgq.at[i], s2_send.at[i], s2_recv.at[i], peer)

    def gain_new():
        for i in range(3):
            got(pgq.at[i], s2_send.at[i], s2_recv.at[i])
        gg = (pgs[...] + pgq[0] + pgq[1] + pgq[2]).sum(axis=0, keepdims=True)
        gquad[0] = jnp.broadcast_to(gall[x, 0:1, :] - RATE_GAIN * gg, gplace.shape)
        window = pl.ds(pl.multiple_of((y * 2 + c) * LANES, LANES), 2 * LANES)
        ngain[...] = gquad[0, :, window].astype(BF16).astype(F32)
        send(ngain, ogain, zg_send, zg_recv, at(x, y, c, dst_r))

    got(a.at[rows(x * 2 + sib)], sib_send.at[0], sib_recv.at[0])
    for px, base in ((left, 1), (right, 3), (far, 5)):
        for h in (0, 1):
            got(a.at[rows(px * 2 + sib, 64 * h, 64)], sib_send.at[base + h], sib_recv.at[base + h])
    got_gradients(0)
    lax.fori_loop(0, NCH, theirs, 0)
    got_gradients(1)

    def zcopy(j):
        slot, target = j, dst_r
        if longs:
            early = j % 2 * (j < 2 * longs)
            slot = j + early * (NCH + j // 2 - j)
            target = dst_r + early * (via_r - dst_r)
        return remote(new.at[j], other.at[slot], z_send.at[j], z_recv.at[slot], at(x, y, c, target))

    def update(j):
        part = jnp.dot(gt[pl.ds(my_rows, C), :], a[:, chunk(j)], preferred_element_type=F32)
        ycopy(j).wait()
        grad = part * factor + yrecv[j].astype(F32)
        new[j] = (wt[columns(y, c), chunk(j)].astype(F32) - RATE_WEIGHT * grad).astype(BF16)
        zcopy(j).start()

    def update_beside(j, _):
        update(j)
        token_rows(j)
        return 0

    def update_alone(j, _):
        update(j)
        return 0

    lax.fori_loop(0, 4, update_beside, 0)
    gain_sums()
    lax.fori_loop(4, 7, update_alone, 0)
    gain_quad()
    lax.fori_loop(7, NCH, update_alone, 0)
    gain_new()

    for i in range(longs):
        got(other.at[NCH + i], z_send.at[0], z_recv.at[NCH + i])
        j = 2 * i + 1
        send(other.at[NCH + i], other.at[j], v_send.at[i], z_recv.at[j], at(x, y, c, via_r))

    def store_mixed(j):
        return pltpu.make_async_copy(mixed.at[j], mixed_out.at[:, chunk(j)], out_sem.at[2 + j])

    def mix(n, _):
        j = (n + 4) % NCH
        got(other.at[j], z_send.at[0], z_recv.at[j])
        mixed[j] = (0.5 * (new[j].astype(F32) + other[j].astype(F32))).astype(BF16)
        store_mixed(j).start()
        return 0

    lax.fori_loop(0, NCH, mix, 0)
    got(ogain, zg_send, zg_recv)
    mean = 0.5 * (ngain[...] + ogain[...])
    turned = pltpu.roll(mean, (2 * LANES - (y * 2 + c) * 32) % (2 * LANES), 1)
    mixed_gain_out[...] = turned[0:1, 0:C].astype(BF16)

    def sent(n, _):
        cp, _, _, mine = gradient_copy(n)

        @pl.when(jnp.logical_not(mine))
        def _():
            cp.wait_send()

        return 0

    lax.fori_loop(0, 16, sent, 0)

    def finished(j, _):
        zcopy(j).wait_send()
        store_mixed(j).wait()
        return 0

    lax.fori_loop(0, NCH, finished, 0)
    store_n.wait()
    store_g.wait()
    for cp in sends:
        cp.wait_send()


def fused(residual, attention, weight, gain, cotangent, level):
    longs = LONGS.get(2**level, 0)
    dma = pltpu.SemaphoreType.DMA
    vm = pltpu.VMEM
    scratch = [
        vm((1, C), BF16),
        vm((8 * T, D), BF16),
        vm((Q, D), BF16),
        vm((T, D), BF16),
        vm((T, D), BF16),
        vm((D, T), BF16),
        vm((D, T), F32),
        vm((4, Q, T), BF16),
        vm((D, T), BF16),
        vm((D, T), BF16),
        vm((2 * C, 8 * T), BF16),
        vm((T, D), BF16),
        vm((T, D), BF16),
        vm((NCH, C, CHUNK), BF16),
        vm((NCH, C, CHUNK), BF16),
        vm((NCH, C, CHUNK), BF16),
        vm((NCH + longs, C, CHUNK), BF16),
        vm((NCH, C, CHUNK), BF16),
        vm((8, Q), F32),
        vm((4, 8, Q), F32),
        vm((4, 8, Q), F32),
        vm((4, 8, Q), F32),
        vm((3, 8, Q), F32),
        vm((8, Q), F32),
        vm((3, 8, Q), F32),
        vm((8, 2 * LANES), F32),
        vm((8, 2 * LANES), F32),
        dma((5,)), dma((2 + NCH,)),
        dma((3, 2)), dma((3, 2)), dma((7,)), dma((7,)), dma((5,)), dma((5,)),
        dma((3,)), dma((3,)), dma((3,)), dma((3,)),
        dma((4, 2)), dma((4, 2)), dma((16,)), dma((8, 2)),
        dma((3,)), dma((3,)), dma((3,)), dma((3,)),
        dma((NCH,)), dma((NCH,)), dma((NCH,)), dma((NCH + longs,)),
        dma((max(longs, 1),)), dma(()), dma(()),
    ]
    hbm = pl.BlockSpec(memory_space=pl.ANY)
    vmem = pl.BlockSpec(memory_space=pltpu.VMEM)
    return pl.pallas_call(
        partial(kernel, 2**level, longs),
        out_shape=(
            jax.ShapeDtypeStruct((T, D), BF16),
            jax.ShapeDtypeStruct((T, D), BF16),
            jax.ShapeDtypeStruct((C, D), BF16),
            jax.ShapeDtypeStruct((1, C), BF16),
        ),
        in_specs=[pl.BlockSpec(memory_space=pltpu.HBM)] * 5,
        out_specs=(hbm, hbm, hbm, vmem),
        scratch_shapes=scratch,
        compiler_params=pltpu.CompilerParams(
            collective_id=level, has_side_effects=True, vmem_limit_bytes=56 * 2**20
        ),
        cost_estimate=pl.CostEstimate(flops=4 * 1024 * 320 * D, bytes_accessed=8 * 2**20, transcendentals=0),
        name=f"replica_step_{level}",
    )(attention, residual, cotangent, weight, gain)


def hand_over(*refs):
    *pairs, sems = refs
    half = len(pairs) // 2
    copies = [
        pltpu.make_async_copy(src, dst, sems.at[i])
        for i, (src, dst) in enumerate(zip(pairs[:half], pairs[half:]))
    ]
    for cp in copies:
        cp.start()
    for cp in copies:
        cp.wait()


def in_place(*results):
    anywhere = pl.BlockSpec(memory_space=pl.ANY)
    return pl.pallas_call(
        hand_over,
        out_shape=tuple(jax.ShapeDtypeStruct(v.shape, v.dtype) for v in results),
        in_specs=[anywhere] * len(results),
        out_specs=(pl.BlockSpec(memory_space=pltpu.HBM),) * len(results),
        scratch_shapes=[pltpu.SemaphoreType.DMA((len(results),))],
        name="hand_over",
    )(*results)


def body(residual, attention, out_weight, norm_gain, cotangent, step_index):
    hop_count = lax.axis_size("replica").bit_length() - 1
    args = (residual[0], attention[0], out_weight[0].T, norm_gain, cotangent[0])
    branches = [lambda ops, level=level: fused(*ops, level) for level in range(hop_count)]
    normed, grad, mixed_t, mixed_gain = lax.switch(step_index[0] % hop_count, branches, args)
    normed, grad, mixed_t, mixed_gain = in_place(normed, grad, mixed_t, mixed_gain)
    return normed[None], grad[None], mixed_t.T[None], mixed_gain


def solution(mesh):
    return jax.shard_map(
        body,
        mesh=mesh,
        in_specs=(
            P("replica", "fsdp", None),
            P("replica", "fsdp", None),
            P("replica", None, "fsdp"),
            P("replica", "fsdp"),
            P("replica", "fsdp", None),
            P(),
        ),
        out_specs=(
            P("replica", "fsdp", None),
            P("replica", "fsdp", None),
            P("replica", None, "fsdp"),
            P("replica", "fsdp"),
        ),
        check_vma=False,
    )
```

```python
from functools import partial
import math

import jax
import jax.numpy as jnp
from jax import lax
from jax.experimental import pallas as pl
from jax.experimental.pallas import tpu as pltpu
from jax.sharding import PartitionSpec as P

EPSILON = 1e-05
RATE_WEIGHT = 0.2
RATE_GAIN = 0.005
MESH = pl.DeviceIdType.MESH
F32 = jnp.float32
BF16 = jnp.bfloat16

D = 2560
T = 128
C = 160
Q = 640
LANES = 128
CHUNK = 256
NCH = D // CHUNK
AHEAD = 4
LONGS = {8: 2}


def kernel(
    distance, longs,
    att, res, cot, weight, gain,
    normed_out, grad_out, mixed_out, mixed_gain_out,
    gain_in, a, wt, rbuf, cbuf, res_t, gn_t, pts, ptr, gts, gt, nbuf, gbuf,
    ysend, yrecv, new, other,
    gplace, gquad, gall, pg, pgx, pgs, pgq, ngain, ogain,
    load_sem, out_sem,
    a_send, a_recv, sib_send, sib_recv, w_send, w_recv,
    g1_send, g1_recv, g2_send, g2_recv,
    p_send, p_recv, t_send, t_recv, s1_send, s1_recv, s2_send, s2_recv,
    y_send, y_recv, z_send, z_recv, v_send, zg_send, zg_recv,
):
    r = lax.axis_index("replica")
    f = lax.axis_index("fsdp")
    replicas = lax.axis_size("replica")
    chip_x, chip_y, c = f // 4, (f // 2) % 2, f % 2
    paired = distance == 1
    x, y = chip_x, chip_y
    if paired:
        edge = (chip_x + 1) // 2 % 2
        x, y = edge * 2 + (chip_y + edge) % 2, chip_x // 2
    s = x * 2 + c
    sib = 1 - c
    factor = 1.0 / math.sqrt(D)

    def block(px, py, pc):
        if paired:
            return (py * 3 + px // 2 * (1 - 2 * py)) * 4 + (px + px // 2) % 2 * 2 + pc
        return px * 4 + py * 2 + pc

    def at(px, py, pc, pr=r):
        return (pr, block(px, py, pc))

    def chip(px, py, pc):
        return (r, px % 4 * 4 + py * 2 + pc)

    def rx(step):
        return (x + step) % 4

    def remote(src, dst, ss, rs, target):
        return pltpu.make_async_remote_copy(
            src_ref=src, dst_ref=dst, send_sem=ss, recv_sem=rs, device_id=target, device_id_type=MESH
        )

    sends = []

    def send(src, dst, ss, rs, target):
        cp = remote(src, dst, ss, rs, target)
        cp.start()
        sends.append(cp)

    def got(ref, ss, rs):
        remote(ref, ref, ss, rs, at(rx(1), y, c)).wait_recv()

    def rows(slot, start=0, size=T):
        return pl.ds(pl.multiple_of(slot * T + start, 64), size)

    my_rows = pl.multiple_of(y * C, 32)
    peer_rows = pl.multiple_of((1 - y) * C, 32)

    def columns(py, pc, start=0, size=C):
        return pl.ds(pl.multiple_of((py * 2 + pc) * C + start, 16), size)

    load_a = pltpu.make_async_copy(att, a.at[rows(s)], load_sem.at[0])
    load_w = pltpu.make_async_copy(weight, wt.at[columns(y, c)], load_sem.at[1])
    load_r = pltpu.make_async_copy(res, rbuf, load_sem.at[2])
    load_c = pltpu.make_async_copy(cot, cbuf, load_sem.at[3])
    load_g = pltpu.make_async_copy(gain, gain_in, load_sem.at[4])
    for cp in (load_g, load_a, load_w, load_r, load_c):
        cp.start()

    leg = (replicas - distance) // 2
    dst_r = (r + distance) % replicas
    src_r = (r + replicas - distance) % replicas
    via_r = (r + replicas - leg) % replicas
    peers = [at(rx(k), y, c) for k in (1, 2, 3)] + [at(rx(k), y, sib) for k in range(4)]
    peers += [at(x, 1 - y, c), chip(chip_x + 2, chip_y, c) if paired else at(x, 1 - y, sib)]
    peers.append(at(x, y, c, dst_r))
    if 2 * distance != replicas:
        peers.append(at(x, y, c, src_r))
    if longs:
        peers += [at(x, y, c, via_r), at(x, y, c, (r + leg) % replicas)]
    barrier = pltpu.get_barrier_semaphore()
    for peer in peers:
        pl.semaphore_signal(barrier, inc=1, device_id=peer, device_id_type=MESH)

    gplace[...] = jnp.zeros(gplace.shape, F32)
    load_g.wait()
    gplace[:, 0:C] = jnp.broadcast_to(gain_in[...].astype(F32), (8, C))
    gplace[...] = pltpu.roll(gplace[...], (chip_y * 2 + c) * C, 1)
    gquad[0] = gplace[...]
    load_a.wait()
    load_w.wait()
    pl.semaphore_wait(barrier, len(peers))

    quad = [chip(chip_x, chip_y, sib), chip(chip_x, 1 - chip_y, c), chip(chip_x, 1 - chip_y, sib)]
    for i, peer in enumerate(quad):
        send(gplace, gquad.at[1 + i], g1_send.at[i], g1_recv.at[i], peer)

    left, right, far = rx(3), rx(1), rx(2)
    for h in (0, 1):
        span = rows(s, 64 * h, 64)
        send(a.at[span], a.at[span], a_send.at[0, h], a_recv.at[0, h], at(right, y, c))
        h2 = 1 - h
        span = rows(s, 64 * h2, 64)
        send(a.at[span], a.at[span], a_send.at[1, h2], a_recv.at[1, h2], at(left, y, c))
    for h in (0, 1):
        span = columns(y, c, 80 * h, 80)
        send(wt.at[span], wt.at[span], w_send.at[h], w_recv.at[h], at(x, 1 - y, c))
    send(wt.at[columns(y, c)], wt.at[columns(y, c)], w_send.at[2], w_recv.at[2], at(x, y, sib))
    send(a.at[rows(s)], a.at[rows(s)], sib_send.at[0], sib_recv.at[0], at(x, y, sib))

    load_r.wait()
    load_c.wait()

    def turn_res(k, _):
        k0 = pl.multiple_of(k * LANES, LANES)
        res_t[pl.ds(k0, LANES), :] = rbuf[:, pl.ds(k0, LANES)].T
        return 0

    lax.fori_loop(0, D // LANES, turn_res, 0)

    for i in range(3):
        got(gquad.at[1 + i], g1_send.at[i], g1_recv.at[i])
    gall[chip_x] = gquad[0] + gquad[1] + gquad[2] + gquad[3]
    for i, k in enumerate((1, 2, 3)):
        mine = gall.at[chip_x]
        send(mine, mine, g2_send.at[i], g2_recv.at[i], chip(chip_x + k, chip_y, c))

    def projected(px, py):
        start = pl.multiple_of(py * 2 * C, 64)
        out = lax.dot_general(
            wt[pl.ds(start, 2 * C), :], a[rows(px * 2 + c), :], (((1,), (1,)), ((), ())),
            preferred_element_type=F32,
        )
        pts[px, pl.ds(start, 2 * C), :] = (out * factor).astype(BF16)

    def feature_rows(px, py, pc):
        return pl.ds(pl.multiple_of(block(px, py, pc) * C, 32), C)

    def half_rows(px, py):
        return pl.ds(pl.multiple_of(block(px, py, 0) * C, 64), 2 * C)

    def hand_out(step, px, i):
        py = y if i == 0 else 1 - y
        src = pts.at[px, pl.ds(pl.multiple_of(py * 2 * C, 64), 2 * C)]
        span = half_rows(x, py)
        if step == 0:
            ptr[span, :] = src[...]
        else:
            send(src, ptr.at[span], p_send.at[step, i], p_recv.at[x, i], at(px, y, c))

    def forward(slot, h, i):
        span = rows(slot, 64 * h, 64)
        send(a.at[span], a.at[span], sib_send.at[i], sib_recv.at[i], at(x, y, sib))

    def pass_on(slot, h, target):
        span = rows(slot, 64 * h, 64)
        send(a.at[span], a.at[span], a_send.at[2, h], a_recv.at[2, h], target)

    got(wt.at[columns(y, sib)], w_send.at[2], w_recv.at[2])
    projected(x, y)
    hand_out(0, x, 0)

    left_c, right_c, far_c = left * 2 + c, right * 2 + c, far * 2 + c
    got(a.at[rows(left_c, 0, 64)], a_send.at[0, 0], a_recv.at[0, 0])
    pass_on(left_c, 0, at(right, y, c))
    got(a.at[rows(right_c, 64, 64)], a_send.at[1, 1], a_recv.at[1, 1])
    pass_on(right_c, 1, at(left, y, c))
    forward(left_c, 0, 1)
    forward(right_c, 1, 4)
    got(a.at[rows(left_c, 64, 64)], a_send.at[0, 1], a_recv.at[0, 1])
    forward(left_c, 1, 2)
    got(a.at[rows(right_c, 0, 64)], a_send.at[1, 0], a_recv.at[1, 0])
    forward(right_c, 0, 3)

    for i, k in enumerate((3, 2, 1)):
        got(gall.at[(chip_x + k) % 4], g2_send.at[i], g2_recv.at[i])
    def turn_cot(n, _):
        span = pl.ds(pl.multiple_of(n * LANES, LANES), LANES)
        row = gall[n // 5, 0:1, pl.ds(pl.multiple_of(n % 5 * LANES, LANES), LANES)]
        gn_t[span, :] = (cbuf[:, span].astype(F32) * row).T
        return 0

    lax.fori_loop(0, D // LANES, turn_cot, 0)

    def near_blocks(n, _):
        projected((x + 3 + 2 * n) % 4, y)
        return 0

    lax.fori_loop(0, 2, near_blocks, 0)
    hand_out(3, left, 0)
    hand_out(1, right, 0)

    for h in (0, 1):
        span = columns(1 - y, c, 80 * h, 80)
        got(wt.at[span], w_send.at[h], w_recv.at[h])
        send(wt.at[span], wt.at[span], w_send.at[3 + h], w_recv.at[3 + h], at(x, y, sib))
    for h in (0, 1):
        got(wt.at[columns(1 - y, sib, 80 * h, 80)], w_send.at[3 + h], w_recv.at[3 + h])

    def near_again(n, _):
        projected((x + 3 + n) % 4, 1 - y)
        return 0

    lax.fori_loop(0, 3, near_again, 0)
    hand_out(3, left, 1)
    hand_out(1, right, 1)
    hand_out(0, x, 1)
    for h in (0, 1):
        got(a.at[rows(far_c, 64 * h, 64)], a_send.at[2, h], a_recv.at[2, h])

    projected(far, y)
    hand_out(2, far, 0)
    projected(far, 1 - y)
    hand_out(2, far, 1)
    for h in (0, 1):
        forward(far_c, h, 5 + h)

    def folded(v):
        return v.reshape(v.shape[0] // 8, 8, T).sum(axis=0)

    def stats(n, carry):
        ss, gs = carry
        span = feature_rows((x + 3 + n // 4) % 4, n % 4 // 2, n % 2)
        sm = res_t[span, :].astype(F32) + ptr[span, :].astype(F32)
        return ss + folded(sm * sm), gs + folded(sm * gn_t[span, :])

    def got_features(step):
        for i in (0, 1):
            px, py = rx(step), (y if i == 0 else 1 - y)
            got(ptr.at[half_rows(px, py)], p_send.at[step, i], p_recv.at[px, i])

    zero = jnp.zeros((8, T), F32)
    got_features(3)
    got_features(1)
    sums = lax.fori_loop(0, 12, stats, (zero, zero))
    got_features(2)
    ss, gs = lax.fori_loop(12, 16, stats, sums)
    inv = lax.rsqrt(ss.sum(axis=0, keepdims=True) * (1.0 / D) + EPSILON)
    inner = gs.sum(axis=0, keepdims=True) * (1.0 / D) * inv
    pull = inner * inv * inv

    my_lanes = pl.ds(pl.multiple_of(s * T, T), T)

    def gradient_copy(n):
        m = n % 8
        px, pc = (x + 2 + m // 2) % 4, (c + m) % 2
        py = (y + 1 + n // 8) % 2
        span = feature_rows(px, py, pc)
        land = pl.ds(pl.multiple_of(py * C, 32), C)
        cp = remote(
            gts.at[span], gt.at[land, my_lanes], t_send.at[n], t_recv.at[s, n // 8], at(px, y, pc)
        )
        return cp, span, land, m == 4

    def gradients(n, _):
        cp, span, land, mine = gradient_copy(n)
        sm = res_t[span, :].astype(F32) + ptr[span, :].astype(F32)
        gts[span, :] = (gn_t[span, :] * inv - sm * pull).astype(BF16)

        @pl.when(mine)
        def _():
            gt[land, my_lanes] = gts[span, :]

        @pl.when(jnp.logical_not(mine))
        def _():
            cp.start()

        return 0

    lax.fori_loop(0, 16, gradients, 0)

    def got_gradients(i):
        land = pl.ds(my_rows if i else peer_rows, C)
        for k in (0, 1):
            for step in range(4):
                if k == 0 and step == 0:
                    continue
                slot = rx(step) * 2 + (c if k == 0 else sib)
                lanes = pl.ds(pl.multiple_of(slot * T, T), T)
                got(gt.at[land, lanes], t_send.at[0], t_recv.at[slot, i])

    def chunk(j):
        return pl.ds(pl.multiple_of(j * CHUNK, CHUNK), CHUNK)

    def ycopy(j):
        return remote(ysend.at[j], yrecv.at[j], y_send.at[j], y_recv.at[j], at(x, 1 - y, c))

    def theirs(j, _):
        part = jnp.dot(gt[pl.ds(peer_rows, C), :], a[:, chunk(j)], preferred_element_type=F32)
        ysend[j] = (part * factor).astype(BF16)
        ycopy(j).start()
        return 0

    inv_n = jnp.broadcast_to(inv, (LANES, T)).T
    pull_n = jnp.broadcast_to(pull, (LANES, T)).T

    def token_rows(px):
        def part(k, _):
            span = pl.ds(pl.multiple_of(px * Q + k * LANES, LANES), LANES)
            within = pl.ds(pl.multiple_of(k * LANES, LANES), LANES)
            row = gall[px, 0:1, within]
            sm = rbuf[:, span].astype(F32) + ptr[span, :].T.astype(F32)
            ct = cbuf[:, span].astype(F32)
            nm = sm * inv_n
            nbuf[:, span] = (nm * row).astype(BF16)
            gbuf[:, span] = (ct * row * inv_n - sm * pull_n).astype(BF16)
            pg[px, :, within] = folded(ct * nm)
            return 0

        lax.fori_loop(0, Q // LANES, part, 0)

    store_n = pltpu.make_async_copy(nbuf, normed_out, out_sem.at[0])
    store_g = pltpu.make_async_copy(gbuf, grad_out, out_sem.at[1])

    def gain_sums():
        store_n.start()
        store_g.start()
        for i, k in enumerate((1, 2, 3)):
            px = (chip_x + k) % 4
            send(pg.at[px], pgx.at[i], s1_send.at[i], s1_recv.at[i], chip(px, chip_y, c))

    def gain_quad():
        for i, k in enumerate((3, 2, 1)):
            got(pgx.at[i], s1_send.at[i], s1_recv.at[i])
        pgs[...] = pg[chip_x] + pgx[0] + pgx[1] + pgx[2]
        for i, peer in enumerate(quad):
            send(pgs, pgq.at[i], s2_send.at[i], s2_recv.at[i], peer)

    def gain_new():
        for i in range(3):
            got(pgq.at[i], s2_send.at[i], s2_recv.at[i])
        gg = (pgs[...] + pgq[0] + pgq[1] + pgq[2]).sum(axis=0, keepdims=True)
        gquad[0] = jnp.broadcast_to(gall[chip_x, 0:1, :] - RATE_GAIN * gg, gplace.shape)
        window = pl.ds(pl.multiple_of((chip_y * 2 + c) * LANES, LANES), 2 * LANES)
        ngain[...] = gquad[0, :, window].astype(BF16).astype(F32)
        send(ngain, ogain, zg_send, zg_recv, at(x, y, c, dst_r))

    got(a.at[rows(x * 2 + sib)], sib_send.at[0], sib_recv.at[0])
    for px, base in ((left, 1), (right, 3), (far, 5)):
        for h in (0, 1):
            got(a.at[rows(px * 2 + sib, 64 * h, 64)], sib_send.at[base + h], sib_recv.at[base + h])
    got_gradients(0)
    lax.fori_loop(0, AHEAD, theirs, 0)
    got_gradients(1)

    def zcopy(j):
        slot, target = j, dst_r
        if longs:
            early = j % 2 * (j < 2 * longs)
            slot = j + early * (NCH + j // 2 - j)
            target = dst_r + early * (via_r - dst_r)
        return remote(new.at[j], other.at[slot], z_send.at[j], z_recv.at[slot], at(x, y, c, target))

    def update(j):
        part = jnp.dot(gt[pl.ds(my_rows, C), :], a[:, chunk(j)], preferred_element_type=F32)
        ycopy(j).wait()
        grad = part * factor + yrecv[j].astype(F32)
        new[j] = (wt[columns(y, c), chunk(j)].astype(F32) - RATE_WEIGHT * grad).astype(BF16)
        zcopy(j).start()

    def update_beside(j, _):
        theirs(j + AHEAD, 0)
        update(j)
        token_rows(j)
        return 0

    def update_ahead(j, _):
        theirs(j + AHEAD, 0)
        update(j)
        return 0

    def update_alone(j, _):
        update(j)
        return 0

    lax.fori_loop(0, 4, update_beside, 0)
    gain_sums()
    lax.fori_loop(4, NCH - AHEAD, update_ahead, 0)
    gain_quad()
    lax.fori_loop(NCH - AHEAD, NCH, update_alone, 0)
    for cp in sends:
        cp.wait_send()
    sends.clear()

    def sent(n, _):
        cp, _, _, mine = gradient_copy(n)

        @pl.when(jnp.logical_not(mine))
        def _():
            cp.wait_send()

        return 0

    lax.fori_loop(0, 16, sent, 0)
    gain_new()

    for i in range(longs):
        got(other.at[NCH + i], z_send.at[0], z_recv.at[NCH + i])
        j = 2 * i + 1
        send(other.at[NCH + i], other.at[j], v_send.at[i], z_recv.at[j], at(x, y, c, via_r))

    def mix(n, _):
        j = (n + 4) % NCH
        got(other.at[j], z_send.at[0], z_recv.at[j])
        mixed_out[:, chunk(j)] = (0.5 * (new[j].astype(F32) + other[j].astype(F32))).astype(BF16)
        zcopy(j).wait_send()
        return 0

    lax.fori_loop(0, NCH, mix, 0)
    got(ogain, zg_send, zg_recv)
    mean = 0.5 * (ngain[...] + ogain[...])
    turned = pltpu.roll(mean, (2 * LANES - (chip_y * 2 + c) * 32) % (2 * LANES), 1)
    mixed_gain_out[...] = turned[0:1, 0:C].astype(BF16)

    store_n.wait()
    store_g.wait()
    for cp in sends:
        cp.wait_send()


def fused(residual, attention, weight, gain, cotangent, level):
    longs = LONGS.get(2**level, 0)
    dma = pltpu.SemaphoreType.DMA
    vm = pltpu.VMEM
    scratch = [
        vm((1, C), BF16),
        vm((8 * T, D), BF16),
        vm((Q, D), BF16),
        vm((T, D), BF16),
        vm((T, D), BF16),
        vm((D, T), BF16),
        vm((D, T), F32),
        vm((4, Q, T), BF16),
        vm((D, T), BF16),
        vm((D, T), BF16),
        vm((2 * C, 8 * T), BF16),
        vm((T, D), BF16),
        vm((T, D), BF16),
        vm((NCH, C, CHUNK), BF16),
        vm((NCH, C, CHUNK), BF16),
        vm((NCH, C, CHUNK), BF16),
        vm((NCH + longs, C, CHUNK), BF16),
        vm((8, Q), F32),
        vm((4, 8, Q), F32),
        vm((4, 8, Q), F32),
        vm((4, 8, Q), F32),
        vm((3, 8, Q), F32),
        vm((8, Q), F32),
        vm((3, 8, Q), F32),
        vm((8, 2 * LANES), F32),
        vm((8, 2 * LANES), F32),
        dma((5,)), dma((2,)),
        dma((3, 2)), dma((3, 2)), dma((7,)), dma((7,)), dma((5,)), dma((5,)),
        dma((3,)), dma((3,)), dma((3,)), dma((3,)),
        dma((4, 2)), dma((4, 2)), dma((16,)), dma((8, 2)),
        dma((3,)), dma((3,)), dma((3,)), dma((3,)),
        dma((NCH,)), dma((NCH,)), dma((NCH,)), dma((NCH + longs,)),
        dma((max(longs, 1),)), dma(()), dma(()),
    ]
    hbm = pl.BlockSpec(memory_space=pl.ANY)
    vmem = pl.BlockSpec(memory_space=pltpu.VMEM)
    return pl.pallas_call(
        partial(kernel, 2**level, longs),
        out_shape=(
            jax.ShapeDtypeStruct((T, D), BF16),
            jax.ShapeDtypeStruct((T, D), BF16),
            jax.ShapeDtypeStruct((C, D), BF16),
            jax.ShapeDtypeStruct((1, C), BF16),
        ),
        in_specs=[pl.BlockSpec(memory_space=pltpu.HBM)] * 5,
        out_specs=(hbm, hbm, vmem, vmem),
        scratch_shapes=scratch,
        compiler_params=pltpu.CompilerParams(
            collective_id=level, has_side_effects=True, vmem_limit_bytes=56 * 2**20
        ),
        cost_estimate=pl.CostEstimate(flops=4 * 1024 * 320 * D, bytes_accessed=8 * 2**20, transcendentals=0),
        name=f"replica_step_{level}",
    )(attention, residual, cotangent, weight, gain)


def hand_over(*refs):
    *pairs, sems = refs
    half = len(pairs) // 2
    copies = [
        pltpu.make_async_copy(src, dst, sems.at[i])
        for i, (src, dst) in enumerate(zip(pairs[:half], pairs[half:]))
    ]
    for cp in copies:
        cp.start()
    for cp in copies:
        cp.wait()


def in_place(*results):
    anywhere = pl.BlockSpec(memory_space=pl.ANY)
    return pl.pallas_call(
        hand_over,
        out_shape=tuple(jax.ShapeDtypeStruct(v.shape, v.dtype) for v in results),
        in_specs=[anywhere] * len(results),
        out_specs=(pl.BlockSpec(memory_space=pltpu.HBM),) * len(results),
        scratch_shapes=[pltpu.SemaphoreType.DMA((len(results),))],
        name="hand_over",
    )(*results)


def body(residual, attention, out_weight, norm_gain, cotangent, step_index):
    hop_count = lax.axis_size("replica").bit_length() - 1
    args = (residual[0], attention[0], out_weight[0].T, norm_gain, cotangent[0])
    branches = [lambda ops, level=level: fused(*ops, level) for level in range(hop_count)]
    normed, grad, mixed_t, mixed_gain = lax.switch(step_index[0] % hop_count, branches, args)
    normed, grad, mixed_t, mixed_gain = in_place(normed, grad, mixed_t, mixed_gain)
    return normed[None], grad[None], mixed_t.T[None], mixed_gain


def solution(mesh):
    return jax.shard_map(
        body,
        mesh=mesh,
        in_specs=(
            P("replica", "fsdp", None),
            P("replica", "fsdp", None),
            P("replica", None, "fsdp"),
            P("replica", "fsdp"),
            P("replica", "fsdp", None),
            P(),
        ),
        out_specs=(
            P("replica", "fsdp", None),
            P("replica", "fsdp", None),
            P("replica", None, "fsdp"),
            P("replica", "fsdp"),
        ),
        check_vma=False,
    )
```

```python
from functools import partial
import math

import jax
import jax.numpy as jnp
from jax import lax
from jax.experimental import pallas as pl
from jax.experimental.pallas import tpu as pltpu
from jax.sharding import PartitionSpec as P

EPSILON = 1e-05
RATE_WEIGHT = 0.2
RATE_GAIN = 0.005
MESH = pl.DeviceIdType.MESH
F32 = jnp.float32
BF16 = jnp.bfloat16

D = 2560
T = 128
C = 160
Q = 640
LANES = 128
CHUNK = 256
NCH = D // CHUNK
PIECE = 32
AHEAD = 4
LONGS = {8: 2}


def kernel(
    distance, longs,
    att, res, cot, weight, gain,
    normed_out, grad_out, mixed_out, mixed_gain_out,
    gain_in, a, wt, rbuf, cbuf, res_t, gn_t, pts, ptr, gts, gt, nbuf, gbuf,
    ysend, yrecv, new, other,
    gplace, gquad, gall, pg, pgx, pgs, pgq, ngain, ogain,
    load_sem, out_sem,
    a_send, a_recv, sib_send, sib_recv, w_send, w_recv,
    g1_send, g1_recv, g2_send, g2_recv,
    p_send, p_recv, t_send, t_recv, s1_send, s1_recv, s2_send, s2_recv,
    y_send, y_recv, z_send, z_recv, v_send, zg_send, zg_recv,
):
    r = lax.axis_index("replica")
    f = lax.axis_index("fsdp")
    replicas = lax.axis_size("replica")
    chip_x, chip_y, c = f // 4, (f // 2) % 2, f % 2
    paired = distance == 1
    x, y = chip_x, chip_y
    if paired:
        edge = (chip_x + 1) // 2 % 2
        x, y = edge * 2 + (chip_y + edge) % 2, chip_x // 2
    s = x * 2 + c
    sib = 1 - c
    factor = 1.0 / math.sqrt(D)

    def block(px, py, pc):
        if paired:
            return (py * 3 + px // 2 * (1 - 2 * py)) * 4 + (px + px // 2) % 2 * 2 + pc
        return px * 4 + py * 2 + pc

    def at(px, py, pc, pr=r):
        return (pr, block(px, py, pc))

    def chip(px, py, pc):
        return (r, px % 4 * 4 + py * 2 + pc)

    def rx(step):
        return (x + step) % 4

    def remote(src, dst, ss, rs, target):
        return pltpu.make_async_remote_copy(
            src_ref=src, dst_ref=dst, send_sem=ss, recv_sem=rs, device_id=target, device_id_type=MESH
        )

    sends = []

    def send(src, dst, ss, rs, target):
        cp = remote(src, dst, ss, rs, target)
        cp.start()
        sends.append(cp)

    def got(ref, ss, rs):
        remote(ref, ref, ss, rs, at(rx(1), y, c)).wait_recv()

    def rows(slot, start=0, size=T):
        return pl.ds(pl.multiple_of(slot * T + start, 64), size)

    my_rows = pl.multiple_of(y * C, 32)
    peer_rows = pl.multiple_of((1 - y) * C, 32)

    def columns(py, pc, start=0, size=C):
        return pl.ds(pl.multiple_of((py * 2 + pc) * C + start, 16), size)

    load_a = pltpu.make_async_copy(att, a.at[rows(s)], load_sem.at[0])
    load_w = pltpu.make_async_copy(weight, wt.at[columns(y, c)], load_sem.at[1])
    load_r = pltpu.make_async_copy(res, rbuf, load_sem.at[2])
    load_c = pltpu.make_async_copy(cot, cbuf, load_sem.at[3])
    load_g = pltpu.make_async_copy(gain, gain_in, load_sem.at[4])
    for cp in (load_g, load_a, load_w, load_r, load_c):
        cp.start()

    leg = (replicas - distance) // 2
    dst_r = (r + distance) % replicas
    src_r = (r + replicas - distance) % replicas
    via_r = (r + replicas - leg) % replicas
    peers = [at(rx(k), y, c) for k in (1, 2, 3)] + [at(rx(k), y, sib) for k in range(4)]
    peers += [at(x, 1 - y, c), chip(chip_x + 2, chip_y, c) if paired else at(x, 1 - y, sib)]
    peers.append(at(x, y, c, dst_r))
    if 2 * distance != replicas:
        peers.append(at(x, y, c, src_r))
    if longs:
        peers += [at(x, y, c, via_r), at(x, y, c, (r + leg) % replicas)]
    barrier = pltpu.get_barrier_semaphore()
    for peer in reversed(peers):
        pl.semaphore_signal(barrier, inc=1, device_id=peer, device_id_type=MESH)

    gplace[...] = jnp.zeros(gplace.shape, F32)
    load_g.wait()
    gplace[:, 0:C] = jnp.broadcast_to(gain_in[...].astype(F32), (8, C))
    gplace[...] = pltpu.roll(gplace[...], (chip_y * 2 + c) * C, 1)
    gquad[0] = gplace[...]
    load_a.wait()
    load_w.wait()
    pl.semaphore_wait(barrier, len(peers))

    quad = [chip(chip_x, chip_y, sib), chip(chip_x, 1 - chip_y, c), chip(chip_x, 1 - chip_y, sib)]
    for i, peer in enumerate(quad):
        send(gplace, gquad.at[1 + i], g1_send.at[i], g1_recv.at[i], peer)

    left, right, far = rx(3), rx(1), rx(2)
    for h in (0, 1):
        span = rows(s, 64 * h, 64)
        send(a.at[span], a.at[span], a_send.at[0, h], a_recv.at[0, h], at(right, y, c))
        h2 = 1 - h
        span = rows(s, 64 * h2, 64)
        send(a.at[span], a.at[span], a_send.at[1, h2], a_recv.at[1, h2], at(left, y, c))
    for h in (0, 1):
        span = columns(y, c, 80 * h, 80)
        send(wt.at[span], wt.at[span], w_send.at[h], w_recv.at[h], at(x, 1 - y, c))
    send(wt.at[columns(y, c)], wt.at[columns(y, c)], w_send.at[2], w_recv.at[2], at(x, y, sib))
    send(a.at[rows(s)], a.at[rows(s)], sib_send.at[0], sib_recv.at[0], at(x, y, sib))

    load_r.wait()
    load_c.wait()

    def turn_res(k, _):
        k0 = pl.multiple_of(k * LANES, LANES)
        res_t[pl.ds(k0, LANES), :] = rbuf[:, pl.ds(k0, LANES)].T
        return 0

    lax.fori_loop(0, D // LANES, turn_res, 0)

    for i in range(3):
        got(gquad.at[1 + i], g1_send.at[i], g1_recv.at[i])
    gall[chip_x] = gquad[0] + gquad[1] + gquad[2] + gquad[3]
    for i, k in enumerate((1, 2, 3)):
        mine = gall.at[chip_x]
        send(mine, mine, g2_send.at[i], g2_recv.at[i], chip(chip_x + k, chip_y, c))

    def projected(px, py):
        start = pl.multiple_of(py * 2 * C, 64)
        out = lax.dot_general(
            wt[pl.ds(start, 2 * C), :], a[rows(px * 2 + c), :], (((1,), (1,)), ((), ())),
            preferred_element_type=F32,
        )
        pts[px, pl.ds(start, 2 * C), :] = (out * factor).astype(BF16)

    def feature_rows(px, py, pc):
        return pl.ds(pl.multiple_of(block(px, py, pc) * C, 32), C)

    def half_rows(px, py):
        return pl.ds(pl.multiple_of(block(px, py, 0) * C, 64), 2 * C)

    def hand_out(step, px, i):
        py = y if i == 0 else 1 - y
        src = pts.at[px, pl.ds(pl.multiple_of(py * 2 * C, 64), 2 * C)]
        span = half_rows(x, py)
        if step == 0:
            ptr[span, :] = src[...]
        else:
            send(src, ptr.at[span], p_send.at[step, i], p_recv.at[x, i], at(px, y, c))

    def forward(slot, h, i):
        span = rows(slot, 64 * h, 64)
        send(a.at[span], a.at[span], sib_send.at[i], sib_recv.at[i], at(x, y, sib))

    def pass_on(slot, h, target):
        span = rows(slot, 64 * h, 64)
        send(a.at[span], a.at[span], a_send.at[2, h], a_recv.at[2, h], target)

    got(wt.at[columns(y, sib)], w_send.at[2], w_recv.at[2])
    projected(x, y)
    hand_out(0, x, 0)

    left_c, right_c, far_c = left * 2 + c, right * 2 + c, far * 2 + c
    got(a.at[rows(left_c, 0, 64)], a_send.at[0, 0], a_recv.at[0, 0])
    pass_on(left_c, 0, at(right, y, c))
    got(a.at[rows(right_c, 64, 64)], a_send.at[1, 1], a_recv.at[1, 1])
    pass_on(right_c, 1, at(left, y, c))
    forward(left_c, 0, 1)
    forward(right_c, 1, 4)
    got(a.at[rows(left_c, 64, 64)], a_send.at[0, 1], a_recv.at[0, 1])
    forward(left_c, 1, 2)
    got(a.at[rows(right_c, 0, 64)], a_send.at[1, 0], a_recv.at[1, 0])
    forward(right_c, 0, 3)

    for i, k in enumerate((3, 2, 1)):
        got(gall.at[(chip_x + k) % 4], g2_send.at[i], g2_recv.at[i])
    def turn_cot(n, _):
        span = pl.ds(pl.multiple_of(n * LANES, LANES), LANES)
        row = gall[n // 5, 0:1, pl.ds(pl.multiple_of(n % 5 * LANES, LANES), LANES)]
        gn_t[span, :] = (cbuf[:, span].astype(F32) * row).T
        return 0

    lax.fori_loop(0, D // LANES, turn_cot, 0)

    def near_blocks(n, _):
        projected((x + 3 + 2 * n) % 4, y)
        return 0

    lax.fori_loop(0, 2, near_blocks, 0)
    hand_out(3, left, 0)
    hand_out(1, right, 0)

    for h in (0, 1):
        span = columns(1 - y, c, 80 * h, 80)
        got(wt.at[span], w_send.at[h], w_recv.at[h])
        send(wt.at[span], wt.at[span], w_send.at[3 + h], w_recv.at[3 + h], at(x, y, sib))
    for h in (0, 1):
        got(wt.at[columns(1 - y, sib, 80 * h, 80)], w_send.at[3 + h], w_recv.at[3 + h])

    def near_again(n, _):
        projected((x + 3 + n) % 4, 1 - y)
        return 0

    lax.fori_loop(0, 3, near_again, 0)
    hand_out(3, left, 1)
    hand_out(1, right, 1)
    hand_out(0, x, 1)
    for h in (0, 1):
        got(a.at[rows(far_c, 64 * h, 64)], a_send.at[2, h], a_recv.at[2, h])

    projected(far, y)
    hand_out(2, far, 0)
    projected(far, 1 - y)
    hand_out(2, far, 1)
    for h in (0, 1):
        forward(far_c, h, 5 + h)

    def folded(v):
        return v.reshape(v.shape[0] // 8, 8, T).sum(axis=0)

    def stats(n, carry):
        ss, gs = carry
        span = feature_rows((x + 3 + n // 4) % 4, n % 4 // 2, n % 2)
        sm = res_t[span, :].astype(F32) + ptr[span, :].astype(F32)
        return ss + folded(sm * sm), gs + folded(sm * gn_t[span, :])

    def got_features(step):
        for i in (0, 1):
            px, py = rx(step), (y if i == 0 else 1 - y)
            got(ptr.at[half_rows(px, py)], p_send.at[step, i], p_recv.at[px, i])

    zero = jnp.zeros((8, T), F32)
    got_features(3)
    got_features(1)
    sums = lax.fori_loop(0, 12, stats, (zero, zero))
    got_features(2)
    ss, gs = lax.fori_loop(12, 16, stats, sums)
    inv = lax.rsqrt(ss.sum(axis=0, keepdims=True) * (1.0 / D) + EPSILON)
    inner = gs.sum(axis=0, keepdims=True) * (1.0 / D) * inv
    pull = inner * inv * inv

    my_lanes = pl.ds(pl.multiple_of(s * T, T), T)

    def gradient_copy(n):
        m = n % 8
        px, pc = (x + 2 + m // 2) % 4, (c + m) % 2
        py = (y + 1 + n // 8) % 2
        span = feature_rows(px, py, pc)
        land = pl.ds(pl.multiple_of(py * C, 32), C)
        cp = remote(
            gts.at[span], gt.at[land, my_lanes], t_send.at[n], t_recv.at[s, n // 8], at(px, y, pc)
        )
        return cp, span, land, m == 4

    def gradients(n, _):
        cp, span, land, mine = gradient_copy(n)
        sm = res_t[span, :].astype(F32) + ptr[span, :].astype(F32)
        gts[span, :] = (gn_t[span, :] * inv - sm * pull).astype(BF16)

        @pl.when(mine)
        def _():
            gt[land, my_lanes] = gts[span, :]

        @pl.when(jnp.logical_not(mine))
        def _():
            cp.start()

        return 0

    lax.fori_loop(0, 16, gradients, 0)

    def got_gradients(i):
        land = pl.ds(my_rows if i else peer_rows, C)
        for k in (0, 1):
            for step in range(4):
                if k == 0 and step == 0:
                    continue
                slot = rx(step) * 2 + (c if k == 0 else sib)
                lanes = pl.ds(pl.multiple_of(slot * T, T), T)
                got(gt.at[land, lanes], t_send.at[0], t_recv.at[slot, i])

    def chunk(j):
        return pl.ds(pl.multiple_of(j * CHUNK, CHUNK), CHUNK)

    def ycopy(j):
        return remote(ysend.at[j], yrecv.at[j], y_send.at[j], y_recv.at[j], at(x, 1 - y, c))

    def theirs(j, _):
        part = jnp.dot(gt[pl.ds(peer_rows, C), :], a[:, chunk(j)], preferred_element_type=F32)
        ysend[j] = (part * factor).astype(BF16)
        ycopy(j).start()
        return 0

    inv_n = jnp.broadcast_to(inv, (LANES, T)).T
    pull_n = jnp.broadcast_to(pull, (LANES, T)).T

    def token_rows(px):
        def part(k, _):
            span = pl.ds(pl.multiple_of(px * Q + k * LANES, LANES), LANES)
            within = pl.ds(pl.multiple_of(k * LANES, LANES), LANES)
            row = gall[px, 0:1, within]
            sm = rbuf[:, span].astype(F32) + ptr[span, :].T.astype(F32)
            ct = cbuf[:, span].astype(F32)
            nm = sm * inv_n
            nbuf[:, span] = (nm * row).astype(BF16)
            gbuf[:, span] = (ct * row * inv_n - sm * pull_n).astype(BF16)
            pg[px, :, within] = folded(ct * nm)
            return 0

        lax.fori_loop(0, Q // LANES, part, 0)

    store_n = pltpu.make_async_copy(nbuf, normed_out, out_sem.at[0])
    store_g = pltpu.make_async_copy(gbuf, grad_out, out_sem.at[1])

    def gain_sums():
        store_n.start()
        store_g.start()
        for i, k in enumerate((1, 2, 3)):
            px = (chip_x + k) % 4
            send(pg.at[px], pgx.at[i], s1_send.at[i], s1_recv.at[i], chip(px, chip_y, c))

    def gain_quad():
        for i, k in enumerate((3, 2, 1)):
            got(pgx.at[i], s1_send.at[i], s1_recv.at[i])
        pgs[...] = pg[chip_x] + pgx[0] + pgx[1] + pgx[2]
        for i, peer in enumerate(quad):
            send(pgs, pgq.at[i], s2_send.at[i], s2_recv.at[i], peer)

    def gain_new():
        for i in range(3):
            got(pgq.at[i], s2_send.at[i], s2_recv.at[i])
        gg = (pgs[...] + pgq[0] + pgq[1] + pgq[2]).sum(axis=0, keepdims=True)
        gquad[0] = jnp.broadcast_to(gall[chip_x, 0:1, :] - RATE_GAIN * gg, gplace.shape)
        window = pl.ds(pl.multiple_of((chip_y * 2 + c) * LANES, LANES), 2 * LANES)
        ngain[...] = gquad[0, :, window].astype(BF16).astype(F32)
        send(ngain, ogain, zg_send, zg_recv, at(x, y, c, dst_r))

    got(a.at[rows(x * 2 + sib)], sib_send.at[0], sib_recv.at[0])
    for px, base in ((left, 1), (right, 3), (far, 5)):
        for h in (0, 1):
            got(a.at[rows(px * 2 + sib, 64 * h, 64)], sib_send.at[base + h], sib_recv.at[base + h])
    got_gradients(0)
    lax.fori_loop(0, AHEAD, theirs, 0)
    got_gradients(1)

    def zcopy(j):
        slot, target = j, dst_r
        if longs:
            early = j % 2 * (j < 2 * longs)
            slot = j + early * (NCH + j // 2 - j)
            target = dst_r + early * (via_r - dst_r)
        return remote(new.at[j], other.at[slot], z_send.at[j], z_recv.at[slot], at(x, y, c, target))

    def update(j):
        part = jnp.dot(gt[pl.ds(my_rows, C), :], a[:, chunk(j)], preferred_element_type=F32)
        ycopy(j).wait()
        grad = part * factor + yrecv[j].astype(F32)
        new[j] = (wt[columns(y, c), chunk(j)].astype(F32) - RATE_WEIGHT * grad).astype(BF16)
        zcopy(j).start()

    def update_beside(j, _):
        theirs(j + AHEAD, 0)
        update(j)
        token_rows(j)
        return 0

    def update_ahead(j, _):
        theirs(j + AHEAD, 0)
        update(j)
        return 0

    def update_alone(j, _):
        update(j)
        return 0

    lax.fori_loop(0, 4, update_beside, 0)
    gain_sums()
    lax.fori_loop(4, NCH - AHEAD, update_ahead, 0)
    gain_quad()
    lax.fori_loop(NCH - AHEAD, NCH, update_alone, 0)
    for cp in sends:
        cp.wait_send()
    sends.clear()

    def sent(n, _):
        cp, _, _, mine = gradient_copy(n)

        @pl.when(jnp.logical_not(mine))
        def _():
            cp.wait_send()

        return 0

    lax.fori_loop(0, 16, sent, 0)
    gain_new()

    for i in range(longs):
        got(other.at[NCH + i], z_send.at[0], z_recv.at[NCH + i])
        j = 2 * i + 1
        send(other.at[NCH + i], other.at[j], v_send.at[i], z_recv.at[j], at(x, y, c, via_r))

    def mix(n, _):
        j = (n + 4) % NCH
        got(other.at[j], z_send.at[0], z_recv.at[j])
        mixed_out[:, chunk(j)] = (0.5 * (new[j].astype(F32) + other[j].astype(F32))).astype(BF16)
        zcopy(j).wait_send()
        return 0

    lax.fori_loop(0, NCH, mix, 0)
    got(ogain, zg_send, zg_recv)
    mean = 0.5 * (ngain[...] + ogain[...])
    turned = pltpu.roll(mean, (2 * LANES - (chip_y * 2 + c) * 32) % (2 * LANES), 1)
    mixed_gain_out[...] = turned[0:1, 0:C].astype(BF16)

    store_n.wait()
    store_g.wait()
    for cp in sends:
        cp.wait_send()


def fused(residual, attention, weight, gain, cotangent, level):
    longs = LONGS.get(2**level, 0)
    dma = pltpu.SemaphoreType.DMA
    vm = pltpu.VMEM
    scratch = [
        vm((1, C), BF16),
        vm((8 * T, D), BF16),
        vm((Q, D), BF16),
        vm((T, D), BF16),
        vm((T, D), BF16),
        vm((D, T), BF16),
        vm((D, T), F32),
        vm((4, Q, T), BF16),
        vm((D, T), BF16),
        vm((D, T), BF16),
        vm((2 * C, 8 * T), BF16),
        vm((T, D), BF16),
        vm((T, D), BF16),
        vm((NCH, C, CHUNK), BF16),
        vm((NCH, C, CHUNK), BF16),
        vm((NCH, C, CHUNK), BF16),
        vm((NCH + longs, C, CHUNK), BF16),
        vm((8, Q), F32),
        vm((4, 8, Q), F32),
        vm((4, 8, Q), F32),
        vm((4, 8, Q), F32),
        vm((3, 8, Q), F32),
        vm((8, Q), F32),
        vm((3, 8, Q), F32),
        vm((8, 2 * LANES), F32),
        vm((8, 2 * LANES), F32),
        dma((5,)), dma((2,)),
        dma((3, 2)), dma((3, 2)), dma((7,)), dma((7,)), dma((5,)), dma((5,)),
        dma((3,)), dma((3,)), dma((3,)), dma((3,)),
        dma((4, 2)), dma((4, 2)), dma((16,)), dma((8, 2)),
        dma((3,)), dma((3,)), dma((3,)), dma((3,)),
        dma((NCH,)), dma((NCH,)), dma((NCH,)), dma((NCH + longs,)),
        dma((max(longs, 1),)), dma(()), dma(()),
    ]
    hbm = pl.BlockSpec(memory_space=pl.ANY)
    vmem = pl.BlockSpec(memory_space=pltpu.VMEM)
    return pl.pallas_call(
        partial(kernel, 2**level, longs),
        out_shape=(
            jax.ShapeDtypeStruct((T, D), BF16),
            jax.ShapeDtypeStruct((T, D), BF16),
            jax.ShapeDtypeStruct((C, D), BF16),
            jax.ShapeDtypeStruct((1, C), BF16),
        ),
        in_specs=[pl.BlockSpec(memory_space=pltpu.HBM)] * 5,
        out_specs=(hbm, hbm, vmem, vmem),
        scratch_shapes=scratch,
        compiler_params=pltpu.CompilerParams(
            collective_id=level, has_side_effects=True, vmem_limit_bytes=56 * 2**20
        ),
        cost_estimate=pl.CostEstimate(flops=4 * 1024 * 320 * D, bytes_accessed=8 * 2**20, transcendentals=0),
        name=f"replica_step_{level}",
    )(attention, residual, cotangent, weight, gain)


def hand_over(*refs):
    *pairs, sems = refs
    half = len(pairs) // 2
    parts = []
    for src, dst in zip(pairs[:half], pairs[half:]):
        step = min(PIECE, src.shape[0])
        parts += [(src.at[pl.ds(k, step)], dst.at[pl.ds(k, step)]) for k in range(0, src.shape[0], step)]
    copies = [pltpu.make_async_copy(src, dst, sems.at[i]) for i, (src, dst) in enumerate(parts)]
    for cp in copies:
        cp.start()
    for cp in copies:
        cp.wait()


def in_place(*results):
    anywhere = pl.BlockSpec(memory_space=pl.ANY)
    return pl.pallas_call(
        hand_over,
        out_shape=tuple(jax.ShapeDtypeStruct(v.shape, v.dtype) for v in results),
        in_specs=[anywhere] * len(results),
        out_specs=(pl.BlockSpec(memory_space=pltpu.HBM),) * len(results),
        scratch_shapes=[pltpu.SemaphoreType.DMA((sum(-(-v.shape[0] // PIECE) for v in results),))],
        name="hand_over",
    )(*results)


def body(residual, attention, out_weight, norm_gain, cotangent, step_index):
    hop_count = lax.axis_size("replica").bit_length() - 1
    args = (residual[0], attention[0], out_weight[0].T, norm_gain, cotangent[0])
    branches = [lambda ops, level=level: fused(*ops, level) for level in range(hop_count)]
    normed, grad, mixed_t, mixed_gain = lax.switch(step_index[0] % hop_count, branches, args)
    normed, grad, mixed_t, mixed_gain = in_place(normed, grad, mixed_t, mixed_gain)
    return normed[None], grad[None], mixed_t.T[None], mixed_gain


def solution(mesh):
    return jax.shard_map(
        body,
        mesh=mesh,
        in_specs=(
            P("replica", "fsdp", None),
            P("replica", "fsdp", None),
            P("replica", None, "fsdp"),
            P("replica", "fsdp"),
            P("replica", "fsdp", None),
            P(),
        ),
        out_specs=(
            P("replica", "fsdp", None),
            P("replica", "fsdp", None),
            P("replica", None, "fsdp"),
            P("replica", "fsdp"),
        ),
        check_vma=False,
    )
```
